32 devices in a mesh: wide: 16 (over z, y, x), narrow: 2 (over core).
Axes of the slice: x: 2, y: 2, z: 4, core: 2. Of those that a mesh axis runs over, the one named last changes fastest.
Arguments:
- inputs: bfloat16 [393216, 256], P(('wide', 'narrow')), may hold values from -6 to 6
- input_segments: int32 [393216], P(('wide', 'narrow')), may hold values from 0 to 3, as said below
- latent_segments: int32 [196608], P(('wide', 'narrow')), may hold values from 0 to 3, as said below
- cotangent: bfloat16 [196608, 512], P(('wide', 'narrow')), may hold values from -6 to 6
- latent_array: bfloat16 [1024, 512], P('wide', 'narrow'), may hold values from -6 to 6
- query_gain: bfloat16 [512], replicated, may hold values from 0.25 to 1.75
- query_shift: bfloat16 [512], replicated, may hold values from -1.796875 to 1.796875
- source_gain: bfloat16 [256], replicated, may hold values from 0.25 to 1.75
- source_shift: bfloat16 [256], replicated, may hold values from -1.796875 to 1.796875
- cross_query: bfloat16 [512, 512], P('wide', 'narrow'), may hold values from -0.25 to 0.25
- cross_qbias: bfloat16 [512], replicated, may hold values from -1.796875 to 1.796875
- cross_keyval: bfloat16 [256, 1024], P('wide', 'narrow'), may hold values from -0.375 to 0.375
- cross_vbias: bfloat16 [512], replicated, may hold values from -1.796875 to 1.796875
- cross_output: bfloat16 [512, 512], P('wide', 'narrow'), may hold values from -1.5 to 1.5
- cross_obias: bfloat16 [512], replicated, may hold values from -1.796875 to 1.796875
- self_gain: bfloat16 [512], replicated, may hold values from 0.25 to 1.75
- self_shift: bfloat16 [512], replicated, may hold values from -1.796875 to 1.796875
- self_project: bfloat16 [512, 1536], P('wide', 'narrow'), may hold values from -0.25 to 0.25
- self_qbias: bfloat16 [512], replicated, may hold values from -1.796875 to 1.796875
- self_vbias: bfloat16 [512], replicated, may hold values from -1.796875 to 1.796875
- self_output: bfloat16 [512, 512], P('wide', 'narrow'), may hold values from -1 to 1
- self_obias: bfloat16 [512], replicated, may hold values from -1.796875 to 1.796875
- feed_gain: bfloat16 [512], replicated, may hold values from 0.25 to 1.75
- feed_shift: bfloat16 [512], replicated, may hold values from -1.796875 to 1.796875
- feed_upward: bfloat16 [512, 2048], P('wide', 'narrow'), may hold values from -0.25 to 0.25
- feed_ubias: bfloat16 [2048], replicated, may hold values from -1.796875 to 1.796875
- feed_downward: bfloat16 [2048, 512], P('wide', 'narrow'), may hold values from -0.125 to 0.125
- feed_dbias: bfloat16 [512], replicated, may hold values from -1.796875 to 1.796875
Outputs:
- latents_out: bfloat16 [196608, 512], P(('wide', 'narrow'))
- inputs_grad: float32 [393216, 256], P(('wide', 'narrow'))
- latent_array_grad: float32 [1024, 512], P('wide', 'narrow')
- query_gain_grad: float32 [512], replicated
- query_shift_grad: float32 [512], replicated
- source_gain_grad: float32 [256], replicated
- source_shift_grad: float32 [256], replicated
- cross_query_grad: float32 [512, 512], P('wide', 'narrow')
- cross_qbias_grad: float32 [512], replicated
- cross_keyval_grad: float32 [256, 1024], P('wide', 'narrow')
- cross_vbias_grad: float32 [512], replicated
- cross_output_grad: float32 [512, 512], P('wide', 'narrow')
- cross_obias_grad: float32 [512], replicated
- self_gain_grad: float32 [512], replicated
- self_shift_grad: float32 [512], replicated
- self_project_grad: float32 [512, 1536], P('wide', 'narrow')
- self_qbias_grad: float32 [512], replicated
- self_vbias_grad: float32 [512], replicated
- self_output_grad: float32 [512, 512], P('wide', 'narrow')
- self_obias_grad: float32 [512], replicated
- feed_gain_grad: float32 [512], replicated
- feed_shift_grad: float32 [512], replicated
- feed_upward_grad: float32 [512, 2048], P('wide', 'narrow')
- feed_ubias_grad: float32 [2048], replicated
- feed_downward_grad: float32 [2048, 512], P('wide', 'narrow')
- feed_dbias_grad: float32 [512], replicated
The draws below stay inside these ranges and needn't reach their ends.
Inputs may be any that keep to these rules, and one draw needn't show every extreme that they name: `input_segments`: within each aligned group of 512 input tokens the ids start at 0, never fall, and every id of 0 to 3 occurs. `latent_segments`: within each aligned group of 256 latent rows the ids start at 0, never fall, and every id of 0 to 3 occurs.
All inputs are finite; a program needn't handle non-finite values.
Results may differ from the reference program's by a relative error of at most 0.023.
Values may be sent and summed in bfloat16 or wider, within the bound.
No kernel may reach another device: no remote copies, remote signals or barrier semaphores. Data moves between devices by JAX's collectives and lax.ppermute only.
A program may use at most 448 MiB of HBM per device.

```python
import jax
import jax.numpy as jnp
from jax import lax

D = 512
HEADS = 16
HD = 32
FF = 2048
CIN = 256
G = 4
NL = 256
IN_G = 512
SEGS = 4
SAMP_DEV = 2
SAMPLES = 192
TOK_LAT = 196608
TOK_IN = 393216
LAT_ROWS = 1024


def segment_ids(base_key, group_count, length):
    group_keys = jax.random.split(base_key, group_count)

    def one_group(group_key):
        shuffled = jax.random.permutation(group_key, length - 1) + 1
        cut_points = shuffled[:SEGS - 1]
        places = jnp.arange(length)
        return jnp.sum((places[:, None] >= cut_points[None, :]).astype(jnp.int32), 1).astype(jnp.int32)
    return jax.vmap(one_group)(group_keys).reshape(group_count * length)


def draw_input_segments(key, part):
    key = jax.random.fold_in(key, 11)
    return segment_ids(key, SAMPLES * G, IN_G)


def draw_latent_segments(key, part):
    key = jax.random.fold_in(key, 23)
    return segment_ids(key, SAMPLES * G, NL)


def shard_levels(own_key, extent, shards, smallest, largest):
    def one(axis_at, parts):
        heights = jax.random.uniform(jax.random.fold_in(jax.random.fold_in(own_key, 6), axis_at), (parts,), jnp.float32, smallest / len(shards), largest / len(shards))
        return jnp.repeat(jnp.exp(heights), extent[axis_at] // parts).reshape((-1,) + (1,) * (len(extent) - axis_at - 1))

    loudness = one(*shards[0])
    for cut in shards[1:]:
        loudness = loudness * one(*cut)
    return loudness


def noise(stream_key, dims, scale, most, cuts=(), dtype=jnp.bfloat16):
    values = scale * jax.random.normal(stream_key, dims, jnp.float32)
    if cuts:
        values = values * shard_levels(stream_key, dims, cuts, -0.22, 0.18)
    return jnp.clip(values, -most, most).astype(dtype)


def setup_inputs(seed: int = 0) -> dict:
    keys = jax.random.split(jax.random.key(seed), 29)
    inputs = noise(keys[0], (TOK_IN, CIN), 1.0, 6.0, ((0, 32),))
    input_segments = draw_input_segments(jax.random.fold_in(keys[28], 71), 0)
    latent_segments = draw_latent_segments(jax.random.fold_in(keys[28], 71), 0)
    cotangent = noise(keys[3], (TOK_LAT, D), 1.0, 6.0, ((0, 32),))
    latent_array = noise(keys[4], (LAT_ROWS, D), 1.0, 6.0, ((0, 16), (1, 2)))
    query_gain = jnp.clip(1.0 + 0.15 * jax.random.normal(keys[5], (D,), jnp.float32), 0.25, 1.75).astype(jnp.bfloat16)
    query_shift = noise(keys[6], (D,), 0.3, 1.796875)
    source_gain = jnp.clip(1.0 + 0.15 * jax.random.normal(keys[7], (CIN,), jnp.float32), 0.25, 1.75).astype(jnp.bfloat16)
    source_shift = noise(keys[8], (CIN,), 0.3, 1.796875)
    cross_query = noise(keys[9], (D, D), D ** -0.5, 0.25, ((0, 16), (1, 2)))
    cross_qbias = noise(keys[10], (D,), 0.3, 1.796875)
    cross_keyval = noise(keys[11], (CIN, 2 * D), CIN ** -0.5, 0.375, ((0, 16), (1, 2)))
    cross_vbias = noise(keys[12], (D,), 0.3, 1.796875)
    cross_output = noise(keys[13], (D, D), (D // 32) ** -0.5, 1.5, ((0, 16), (1, 2)))
    cross_obias = noise(keys[14], (D,), 0.3, 1.796875)
    self_gain = jnp.clip(1.0 + 0.15 * jax.random.normal(keys[15], (D,), jnp.float32), 0.25, 1.75).astype(jnp.bfloat16)
    self_shift = noise(keys[16], (D,), 0.3, 1.796875)
    self_project = noise(keys[17], (D, 3 * D), D ** -0.5, 0.25, ((0, 16), (1, 2)))
    self_qbias = noise(keys[18], (D,), 0.3, 1.796875)
    self_vbias = noise(keys[19], (D,), 0.3, 1.796875)
    self_output = noise(keys[20], (D, D), (D // 16) ** -0.5, 1.0, ((0, 16), (1, 2)))
    self_obias = noise(keys[21], (D,), 0.3, 1.796875)
    feed_gain = jnp.clip(1.0 + 0.15 * jax.random.normal(keys[22], (D,), jnp.float32), 0.25, 1.75).astype(jnp.bfloat16)
    feed_shift = noise(keys[23], (D,), 0.3, 1.796875)
    feed_upward = noise(keys[24], (D, FF), D ** -0.5, 0.25, ((0, 16), (1, 2)))
    feed_ubias = noise(keys[25], (FF,), 0.3, 1.796875)
    feed_downward = noise(keys[26], (FF, D), FF ** -0.5, 0.125, ((0, 16), (1, 2)))
    feed_dbias = noise(keys[27], (D,), 0.3, 1.796875)
    return dict(inputs=inputs, input_segments=input_segments, latent_segments=latent_segments, cotangent=cotangent, latent_array=latent_array, query_gain=query_gain, query_shift=query_shift, source_gain=source_gain, source_shift=source_shift, cross_query=cross_query, cross_qbias=cross_qbias, cross_keyval=cross_keyval, cross_vbias=cross_vbias, cross_output=cross_output, cross_obias=cross_obias, self_gain=self_gain, self_shift=self_shift, self_project=self_project, self_qbias=self_qbias, self_vbias=self_vbias, self_output=self_output, self_obias=self_obias, feed_gain=feed_gain, feed_shift=feed_shift, feed_upward=feed_upward, feed_ubias=feed_ubias, feed_downward=feed_downward, feed_dbias=feed_dbias)


@jax.custom_vjp
def low(v):
    return lax.optimization_barrier(v.astype(jnp.bfloat16)).astype(jnp.float32)

@jax.custom_vjp
def low_back(v):
    return v

def low_keep(v):
    return (low(v), None)

def low_pass(kept, grad):
    return (grad,)

def back_keep(v):
    return (v, None)

def back_low(kept, grad):
    return (low(grad),)
low.defvjp(low_keep, low_pass)
low_back.defvjp(back_keep, back_low)
NEG_FILL = -1e+30
EPSILON = 1e-05

def gelu_exact(values_in):
    return 0.5 * values_in * (1.0 + jax.scipy.special.erf(values_in * 0.5 ** 0.5))

def layer_norm(source_rows, gain_vec, shift_vec):
    centered = source_rows - lax.optimization_barrier(jnp.mean(source_rows, -1, keepdims=True))
    normed = centered * lax.rsqrt(lax.optimization_barrier(jnp.mean(centered * centered, -1, keepdims=True)) + EPSILON)
    return normed * gain_vec + shift_vec

def matmul(left, right):
    return jnp.dot(left, right, precision=lax.Precision.HIGHEST)

def attend(queries, key_rows, values, query_seg, key_seg):
    groups = queries.shape[0]
    qheads = queries.reshape(groups, queries.shape[1], HEADS, HD)
    kheads = key_rows.reshape(groups, key_rows.shape[1], HEADS, HD)
    vheads = values.reshape(groups, values.shape[1], HEADS, HD)
    scores = jnp.einsum('gqhd,gkhd->ghqk', qheads, kheads, precision=lax.Precision.HIGHEST) * HD ** (-0.5)
    scores = low_back(scores)
    allowed = query_seg[:, None, :, None] == key_seg[:, None, None, :]
    scores = jnp.where(allowed, scores, NEG_FILL)
    row_max = lax.optimization_barrier(jnp.max(scores, -1, keepdims=True))
    powers = jnp.exp(scores - row_max)
    attn_probs = low(powers / lax.optimization_barrier(jnp.sum(powers, -1, keepdims=True)))
    blended = jnp.einsum('ghqk,gkhd->gqhd', attn_probs, vheads, precision=lax.Precision.HIGHEST)
    return low(low_back(blended.reshape(groups, queries.shape[1], D)))

def step_forward(weights, inputs_step, in_segs, lat_segs):
    latent_array, query_gain, query_shift, source_gain, source_shift, cross_query, cross_qbias, cross_keyval, cross_vbias, cross_output, cross_obias, self_gain, self_shift, self_project, self_qbias, self_vbias, self_output, self_obias, feed_gain, feed_shift, feed_upward, feed_ubias, feed_downward, feed_dbias = weights
    groups = SAMP_DEV * G
    lat_segs = lat_segs.reshape(groups, NL)
    in_segs = in_segs.reshape(groups, IN_G)
    lat_low = low(layer_norm(latent_array, query_gain, query_shift))
    query_rows = low(low_back(matmul(lat_low, cross_query) + cross_qbias))
    query_all = jnp.tile(query_rows.reshape(G, NL, D), (SAMP_DEV, 1, 1))
    source_low = low(layer_norm(inputs_step, source_gain, source_shift))
    kv_bias = jnp.concatenate([jnp.zeros_like(cross_vbias), cross_vbias])
    keyval = low(low_back(matmul(source_low, cross_keyval) + kv_bias)).reshape(groups, IN_G, 2 * D)
    cross_mix = attend(query_all, keyval[:, :, :D], keyval[:, :, D:], lat_segs, in_segs).reshape(groups * NL, D)
    after_cross = jnp.tile(latent_array, (SAMP_DEV, 1)) + low_back(matmul(cross_mix, cross_output) + cross_obias)
    mid_low = low(layer_norm(after_cross, self_gain, self_shift))
    proj_bias = jnp.concatenate([self_qbias, jnp.zeros_like(self_qbias), self_vbias])
    triple = low(low_back(matmul(mid_low, self_project) + proj_bias)).reshape(groups, NL, 3 * D)
    self_mix = attend(triple[:, :, :D], triple[:, :, D:2 * D], triple[:, :, 2 * D:], lat_segs, lat_segs).reshape(groups * NL, D)
    after_self = after_cross + low_back(matmul(self_mix, self_output) + self_obias)
    top_low = low(layer_norm(after_self, feed_gain, feed_shift))
    hidden = low_back(matmul(top_low, feed_upward) + feed_ubias)
    active = low(gelu_exact(hidden))
    return after_self + low_back(matmul(active, feed_downward) + feed_dbias)

def reference(inputs, input_segments, latent_segments, cotangent, latent_array, query_gain, query_shift, source_gain, source_shift, cross_query, cross_qbias, cross_keyval, cross_vbias, cross_output, cross_obias, self_gain, self_shift, self_project, self_qbias, self_vbias, self_output, self_obias, feed_gain, feed_shift, feed_upward, feed_ubias, feed_downward, feed_dbias):
    weights = tuple((weight.astype(jnp.float32) for weight in (latent_array, query_gain, query_shift, source_gain, source_shift, cross_query, cross_qbias, cross_keyval, cross_vbias, cross_output, cross_obias, self_gain, self_shift, self_project, self_qbias, self_vbias, self_output, self_obias, feed_gain, feed_shift, feed_upward, feed_ubias, feed_downward, feed_dbias)))
    step_count = TOK_LAT // (SAMP_DEV * G * NL)
    in_steps = inputs.astype(jnp.float32).reshape(step_count, SAMP_DEV * G * IN_G, CIN)
    in_segs = input_segments.reshape(step_count, SAMP_DEV * G * IN_G)
    lat_segs = latent_segments.reshape(step_count, SAMP_DEV * G * NL)

    def forward(weight_set, in_rows):

        def apply_step(running, slices):
            return (running, jax.checkpoint(step_forward)(weight_set, slices[0], slices[1], slices[2]))
        return lax.scan(apply_step, None, (in_rows, in_segs, lat_segs))[1]
    result, pullback = jax.vjp(forward, weights, in_steps)
    dweights, dinputs = pullback(cotangent.astype(jnp.float32).reshape(result.shape))
    return (result.reshape(TOK_LAT, D).astype(jnp.bfloat16), dinputs.reshape(TOK_IN, CIN), dweights[0], dweights[1], dweights[2], dweights[3], dweights[4], dweights[5], dweights[6], dweights[7], dweights[8], dweights[9], dweights[10], dweights[11], dweights[12], dweights[13], dweights[14], dweights[15], dweights[16], dweights[17], dweights[18], dweights[19], dweights[20], dweights[21], dweights[22], dweights[23])
```

```python
import functools

import jax
import jax.numpy as jnp
from jax import lax
from jax.experimental import pallas as pl
from jax.experimental.pallas import tpu as pltpu
from jax.sharding import PartitionSpec as P

D = 512
HEADS = 16
HD = 32
FF = 2048
CIN = 256
G = 4
NL = 256
IN_G = 512
SEGS = 4
QT = 32
PACK = 256
TILES = NL // QT
PER_STEP = 2
LAT_STEP = PER_STEP * NL
IN_STEP = PER_STEP * IN_G
CROSS_WIDTHS = (128, 192, 256, 384, 512)
SELF_WIDTHS = (128, 192, 256)

F32 = jnp.float32
BF16 = jnp.bfloat16
NEG_FILL = -1e30
EPSILON = 1e-05
SCALE = HD**-0.5
LOG2E = 1.4426950408889634
SCALE2 = SCALE * LOG2E
VMEM_BYTES = 60 * 1024 * 1024

TAIL_RATE = 0.28
TAIL_POLY = (
    0.1165209849818009,
    0.06749547174407416,
    0.2689133347091787,
    -0.23699737809142182,
    0.38987640062523105,
    -0.10580882324798475,
)

ROW_QGAIN, ROW_QSHIFT, ROW_SOURCE, ROW_QBIAS, ROW_VBIAS, ROW_COBIAS = range(6)
ROW_SGAIN, ROW_SSHIFT, ROW_SQBIAS, ROW_SVBIAS, ROW_SOBIAS = range(6, 11)
ROW_FGAIN, ROW_FSHIFT, ROW_UBIAS, ROW_DBIAS = 11, 12, 13, 17
VEC_ROWS = 24


def dot_plain(left, right):
    return lax.dot_general(left, right, (((1,), (0,)), ((), ())), preferred_element_type=F32)


def dot_first(left, right):
    return lax.dot_general(left, right, (((0,), (0,)), ((), ())), preferred_element_type=F32)


def dot_last(left, right):
    return lax.dot_general(left, right, (((1,), (1,)), ((), ())), preferred_element_type=F32)


def over_rows(total, chunk, body):
    def step(index, carry):
        body(pl.ds(pl.multiple_of(index * chunk, chunk), chunk))
        return carry

    lax.fori_loop(0, total // chunk, step, 0)


def norm_forward(rows, gain, shift):
    centered = rows - jnp.mean(rows, -1, keepdims=True)
    rscale = lax.rsqrt(jnp.mean(centered * centered, -1, keepdims=True) + EPSILON)
    normed = centered * rscale
    return normed * gain + shift, normed, rscale


def norm_backward(grad, normed, rscale, gain):
    dnormed = grad * gain
    return rscale * (
        dnormed
        - jnp.mean(dnormed, -1, keepdims=True)
        - normed * jnp.mean(dnormed * normed, -1, keepdims=True)
    )


def column_sum(rows):
    return jnp.sum(rows, 0, keepdims=True)


def gelu_pair(hidden):
    size = jnp.abs(hidden)
    ratio = 1.0 / (1.0 + TAIL_RATE * size)
    bell = jnp.exp2(hidden * hidden * (-0.5 * LOG2E))
    poly = TAIL_POLY[-1] * ratio
    for coefficient in TAIL_POLY[-2::-1]:
        poly = (poly + coefficient) * ratio
    tail = poly * bell
    cdf = jnp.where(hidden >= 0.0, 1.0 - tail, tail)
    return hidden * cdf, cdf + hidden * bell * 0.3989422804014327


def fill_block_mask(mask_ref):
    row_head = lax.broadcasted_iota(jnp.int32, (PACK, PACK), 0) // QT
    lane_head = lax.broadcasted_iota(jnp.int32, (PACK, PACK), 1) // HD
    mask_ref[...] = jnp.where(row_head == lane_head, 1.0, 0.0).astype(BF16)


def block_diagonal(rows, mask):
    return jnp.concatenate([rows] * (PACK // QT), 0) * mask


def take_diagonal(full):
    lane = lax.broadcasted_iota(jnp.int32, (QT, 128), 1)
    columns = []
    for half in range(2):
        base = 128 * half
        picked = full[base : base + QT, base : base + 128]
        for head in range(1, 4):
            row = base + QT * head
            picked = jnp.where(
                lane >= HD * head, full[row : row + QT, base : base + 128], picked
            )
        columns.append(picked)
    return jnp.concatenate(columns, 1)


def segment_at(cuts, place):
    return sum((place >= cut).astype(jnp.int32) for cut in cuts)


def pick(index, values):
    result = values[0]
    for at in range(1, len(values)):
        result = jnp.where(index == at, values[at], result)
    return result


def tile_window(query_cuts, key_cuts, key_count, tile):
    first = segment_at(query_cuts, tile * QT)
    last = segment_at(query_cuts, tile * QT + QT - 1)
    low = pick(first, [0] + key_cuts) // 16 * 16
    return low, pick(last, key_cuts + [key_count]) - low


def in_windows(low, needed, key_count, widths, body):
    smaller = 0
    for width in widths:

        @pl.when((needed > smaller) & (needed <= width))
        def _(width=width):
            body(pl.multiple_of(jnp.minimum(low, key_count - width), 16), width)

        smaller = width


def query_segments(query_cuts, tile):
    lane = lax.broadcasted_iota(jnp.int32, (1, PACK), 1) % QT
    return segment_at(query_cuts, tile * QT + lane)


def fill_key_segments(seg_ref, key_cuts):
    seg_ref[...] = segment_at(key_cuts, lax.broadcasted_iota(jnp.int32, seg_ref.shape, 0))


def allowed_pairs(seg_ref, low, width, query_seg):
    key_seg = seg_ref[pl.ds(low, width), :]
    return jnp.concatenate([key_seg, key_seg], 1) == query_seg


def attend_tile(query, keys, values, allowed, mask):
    scores = jnp.where(allowed, dot_last(keys, block_diagonal(query, mask)), NEG_FILL)
    top = jnp.max(scores, 0, keepdims=True)
    powers = jnp.exp2((scores - top) * SCALE2)
    total = jnp.sum(powers, 0, keepdims=True)
    probs = (powers * (1.0 / total)).astype(BF16)
    mixed = take_diagonal(dot_first(probs, values)).astype(BF16)
    return mixed, probs, top * SCALE2 + jnp.log2(total)


def attend_tile_back(query, keys, values, out_grad, probs, probs_low, mask):
    grad_blocks = block_diagonal(out_grad, mask)
    dprobs = dot_last(values, grad_blocks)
    weighted = probs * dprobs
    delta = jnp.sum(weighted, 0, keepdims=True)
    dscores = (weighted - probs * delta).astype(BF16)
    dvalues = dot_plain(probs_low, grad_blocks)
    dkeys = dot_plain(dscores, block_diagonal(query, mask))
    dquery = take_diagonal(dot_first(dscores, keys))
    return dquery, dkeys, dvalues


def half(part):
    return slice(PACK * part, PACK * part + PACK)


def group_cuts(cuts_ref, group):
    key_cuts = [cuts_ref[group, at] for at in range(SEGS - 1)]
    latent_cuts = [cuts_ref[group, 4 + at] for at in range(SEGS - 1)]
    return key_cuts, latent_cuts


def cross_forward_kernel(
    cuts_ref,
    inputs_ref,
    latent_ref,
    wq_ref,
    wkv_ref,
    wo_ref,
    vec_ref,
    after_ref,
    mix_ref,
    kv_ref,
    lse_ref,
    query_ref,
    source_ref,
    mask_ref,
    seg_ref,
):
    step = pl.program_id(0)

    @pl.when(step == 0)
    def _():
        fill_block_mask(mask_ref)
        low, _, _ = norm_forward(
            latent_ref[...].astype(F32),
            vec_ref[ROW_QGAIN : ROW_QGAIN + 1, :],
            vec_ref[ROW_QSHIFT : ROW_QSHIFT + 1, :],
        )
        query = dot_plain(low.astype(BF16), wq_ref[...])
        query_ref[...] = (query + vec_ref[ROW_QBIAS : ROW_QBIAS + 1, :]).astype(BF16)

    def source_rows(rows):
        low, _, _ = norm_forward(
            inputs_ref[rows, :].astype(F32),
            vec_ref[ROW_SOURCE : ROW_SOURCE + 1, :CIN],
            vec_ref[ROW_SOURCE : ROW_SOURCE + 1, CIN:],
        )
        source_ref[rows, :] = low.astype(BF16)

    over_rows(IN_STEP, 128, source_rows)
    kv_ref[:, :D] = dot_plain(source_ref[...], wkv_ref[:, :D]).astype(BF16)
    kv_ref[:, D:] = (
        dot_plain(source_ref[...], wkv_ref[:, D:]) + vec_ref[ROW_VBIAS : ROW_VBIAS + 1, :]
    ).astype(BF16)

    base = pl.multiple_of(step % (G // PER_STEP) * LAT_STEP, LAT_STEP)
    for member in range(PER_STEP):
        key_cuts, latent_cuts = group_cuts(cuts_ref, step * PER_STEP + member)
        fill_key_segments(seg_ref, key_cuts)

        def tile_body(tile, carry, member=member, key_cuts=key_cuts, latent_cuts=latent_cuts):
            row = pl.multiple_of(member * NL + tile * QT, QT)
            query_seg = query_segments(latent_cuts, tile)
            low, needed = tile_window(latent_cuts, key_cuts, IN_G, tile)

            def window(start, width):
                keys = pl.ds(member * IN_G + start, width)
                allowed = allowed_pairs(seg_ref, start, width, query_seg)
                for part in range(2):
                    mixed, _, lse = attend_tile(
                        query_ref[pl.ds(base + row, QT), half(part)],
                        kv_ref[keys, half(part)],
                        kv_ref[keys, half(part + 2)],
                        allowed,
                        mask_ref[...],
                    )
                    mix_ref[pl.ds(row, QT), half(part)] = mixed
                    lse_ref[pl.ds((member * TILES + tile) * 2 + part, 1), :] = lse

            in_windows(low, needed, IN_G, CROSS_WIDTHS, window)
            return carry

        lax.fori_loop(0, TILES, tile_body, 0)

    after_ref[...] = (
        latent_ref[pl.ds(base, LAT_STEP), :].astype(F32)
        + dot_plain(mix_ref[...], wo_ref[...])
        + vec_ref[ROW_COBIAS : ROW_COBIAS + 1, :]
    )


def middle_kernel(
    cuts_ref,
    after_ref,
    cot_ref,
    wproj_ref,
    wso_ref,
    wup_ref,
    wdn_ref,
    vec_ref,
    out_ref,
    dcross_ref,
    glat_ref,
    small_ref,
    gproj_ref,
    gso_ref,
    gup_ref,
    gdn_ref,
    mask_ref,
    seg_ref,
    hat1_ref,
    rs1_ref,
    low1_ref,
    triple_ref,
    probs_ref,
    mix_ref,
    res_ref,
    hat2_ref,
    rs2_ref,
    low2_ref,
    dtop_ref,
    dso_ref,
    dmix_ref,
    dtriple_ref,
    dkey_ref,
    dvalue_ref,
    aproj_ref,
    aso_ref,
    aup_ref,
    adn_ref,
):
    step = pl.program_id(0)
    last = pl.num_programs(0) - 1

    def vec(row):
        return vec_ref[row : row + 1, :]

    def add_small(row, value):
        small_ref[row : row + 1, :] += value

    @pl.when(step == 0)
    def _():
        fill_block_mask(mask_ref)
        for ref in (glat_ref, small_ref, aproj_ref, aso_ref, aup_ref, adn_ref):
            ref[...] = jnp.zeros(ref.shape, ref.dtype)

    def first_norm(rows):
        low, normed, rscale = norm_forward(after_ref[rows, :], vec(ROW_SGAIN), vec(ROW_SSHIFT))
        low1_ref[rows, :] = low.astype(BF16)
        hat1_ref[rows, :] = normed
        rs1_ref[rows, :] = rscale

    over_rows(LAT_STEP, 64, first_norm)
    for block, bias in enumerate((ROW_SQBIAS, None, ROW_SVBIAS)):
        columns = slice(D * block, D * block + D)
        product = dot_plain(low1_ref[...], wproj_ref[:, columns])
        if bias is not None:
            product = product + vec(bias)
        triple_ref[:, columns] = product.astype(BF16)

    for member in range(PER_STEP):
        _, latent_cuts = group_cuts(cuts_ref, step * PER_STEP + member)
        fill_key_segments(seg_ref, latent_cuts)

        def tile_body(tile, carry, member=member, latent_cuts=latent_cuts):
            row = pl.multiple_of(member * NL + tile * QT, QT)
            query_seg = query_segments(latent_cuts, tile)
            low, needed = tile_window(latent_cuts, latent_cuts, NL, tile)

            def window(start, width):
                keys = pl.ds(member * NL + start, width)
                allowed = allowed_pairs(seg_ref, start, width, query_seg)
                for part in range(2):
                    mixed, probs, _ = attend_tile(
                        triple_ref[pl.ds(row, QT), half(part)],
                        triple_ref[keys, half(part + 2)],
                        triple_ref[keys, half(part + 4)],
                        allowed,
                        mask_ref[...],
                    )
                    mix_ref[pl.ds(row, QT), half(part)] = mixed
                    probs_ref[(member * TILES + tile) * 2 + part, :width, :] = probs

            in_windows(low, needed, NL, SELF_WIDTHS, window)
            return carry

        lax.fori_loop(0, TILES, tile_body, 0)

    res_ref[...] = after_ref[...] + dot_plain(mix_ref[...], wso_ref[...]) + vec(ROW_SOBIAS)

    def second_norm(rows):
        low, normed, rscale = norm_forward(res_ref[rows, :], vec(ROW_FGAIN), vec(ROW_FSHIFT))
        low2_ref[rows, :] = low.astype(BF16)
        hat2_ref[rows, :] = normed
        rs2_ref[rows, :] = rscale

    over_rows(LAT_STEP, 64, second_norm)
    dtop_ref[...] = jnp.zeros(dtop_ref.shape, F32)

    def feed_block(block, carry):
        columns = pl.ds(pl.multiple_of(block * D, D), D)
        hidden = dot_plain(low2_ref[...], wup_ref[:, columns]) + vec_ref[
            pl.ds(ROW_UBIAS + block, 1), :
        ]
        active, slope = gelu_pair(hidden)
        active = active.astype(BF16)
        dhidden = (slope * dot_last(cot_ref[...], wdn_ref[columns, :])).astype(BF16)
        small_ref[pl.ds(ROW_UBIAS + block, 1), :] += column_sum(dhidden.astype(F32))
        res_ref[...] += dot_plain(active, wdn_ref[columns, :])
        adn_ref[columns, :] += dot_first(active, cot_ref[...])
        aup_ref[:, columns] += dot_first(low2_ref[...], dhidden)
        dtop_ref[...] += dot_last(dhidden, wup_ref[:, columns])
        return carry

    lax.fori_loop(0, FF // D, feed_block, 0)

    def after_feed(rows):
        out_ref[rows, :] = (res_ref[rows, :] + vec(ROW_DBIAS)).astype(BF16)
        dtop = dtop_ref[rows, :]
        normed = hat2_ref[rows, :]
        cot = cot_ref[rows, :].astype(F32)
        dafter = cot + norm_backward(dtop, normed, rs2_ref[rows, :], vec(ROW_FGAIN))
        dlow = dafter.astype(BF16)
        res_ref[rows, :] = dafter
        dso_ref[rows, :] = dlow
        add_small(ROW_FGAIN, column_sum(dtop * normed))
        add_small(ROW_FSHIFT, column_sum(dtop))
        add_small(ROW_DBIAS, column_sum(cot))
        add_small(ROW_SOBIAS, column_sum(dlow.astype(F32)))

    over_rows(LAT_STEP, 64, after_feed)
    aso_ref[...] += dot_first(mix_ref[...], dso_ref[...])
    dmix_ref[...] = dot_last(dso_ref[...], wso_ref[...]).astype(BF16)

    for member in range(PER_STEP):
        _, latent_cuts = group_cuts(cuts_ref, step * PER_STEP + member)
        dkey_ref[...] = jnp.zeros(dkey_ref.shape, F32)
        dvalue_ref[...] = jnp.zeros(dvalue_ref.shape, F32)

        def tile_back(tile, carry, member=member, latent_cuts=latent_cuts):
            row = pl.multiple_of(member * NL + tile * QT, QT)
            low, needed = tile_window(latent_cuts, latent_cuts, NL, tile)

            def window(start, width):
                keys = pl.ds(member * NL + start, width)
                for part in range(2):
                    probs_low = probs_ref[(member * TILES + tile) * 2 + part, :width, :]
                    dquery, dkeys, dvalues = attend_tile_back(
                        triple_ref[pl.ds(row, QT), half(part)],
                        triple_ref[keys, half(part + 2)],
                        triple_ref[keys, half(part + 4)],
                        dmix_ref[pl.ds(row, QT), half(part)],
                        probs_low.astype(F32),
                        probs_low,
                        mask_ref[...],
                    )
                    dtriple_ref[pl.ds(row, QT), half(part)] = (dquery * SCALE).astype(BF16)
                    dkey_ref[pl.ds(start, width), half(part)] += dkeys
                    dvalue_ref[pl.ds(start, width), half(part)] += dvalues

            in_windows(low, needed, NL, SELF_WIDTHS, window)
            return carry

        lax.fori_loop(0, TILES, tile_back, 0)
        rows = slice(member * NL, member * NL + NL)
        dtriple_ref[rows, D : 2 * D] = (dkey_ref[...] * SCALE).astype(BF16)
        dtriple_ref[rows, 2 * D :] = dvalue_ref[...].astype(BF16)

    for block in range(3):
        columns = slice(D * block, D * block + D)
        aproj_ref[:, columns] += dot_first(low1_ref[...], dtriple_ref[:, columns])
    add_small(ROW_SQBIAS, column_sum(dtriple_ref[:, :D].astype(F32)))
    add_small(ROW_SVBIAS, column_sum(dtriple_ref[:, 2 * D :].astype(F32)))
    dtop_ref[...] = dot_last(dtriple_ref[...], wproj_ref[...])
    base = step % (G // PER_STEP) * LAT_STEP

    def after_self(rows):
        dmid = dtop_ref[rows, :]
        normed = hat1_ref[rows, :]
        dafter = res_ref[rows, :] + norm_backward(dmid, normed, rs1_ref[rows, :], vec(ROW_SGAIN))
        dcross_ref[rows, :] = dafter.astype(BF16)
        glat_ref[pl.ds(pl.multiple_of(base + rows.start, 64), rows.size), :] += dafter
        add_small(ROW_SGAIN, column_sum(dmid * normed))
        add_small(ROW_SSHIFT, column_sum(dmid))

    over_rows(LAT_STEP, 64, after_self)

    @pl.when(step == last)
    def _():
        gproj_ref[...] = aproj_ref[...].astype(BF16)
        gso_ref[...] = aso_ref[...].astype(BF16)
        gup_ref[...] = aup_ref[...].astype(BF16)
        gdn_ref[...] = adn_ref[...].astype(BF16)


def cross_backward_kernel(
    cuts_ref,
    inputs_ref,
    kv_ref,
    mix_ref,
    lse_ref,
    dcross_ref,
    query_ref,
    latent_ref,
    glat_ref,
    wq_ref,
    wkv_ref,
    wo_ref,
    vec_ref,
    dinput_ref,
    glatout_ref,
    gq_ref,
    gkv_ref,
    go_ref,
    small_ref,
    mask_ref,
    seg_ref,
    source_ref,
    hat_ref,
    rs_ref,
    dmix_ref,
    dkey_ref,
    dvalue_ref,
    dkv_ref,
    dquery_ref,
    akv_ref,
    ao_ref,
):
    step = pl.program_id(0)
    last = pl.num_programs(0) - 1

    def vec(row):
        return vec_ref[row : row + 1, :]

    def add_small(row, value):
        small_ref[row : row + 1, :] += value

    @pl.when(step == 0)
    def _():
        fill_block_mask(mask_ref)
        for ref in (small_ref, dquery_ref, akv_ref, ao_ref):
            ref[...] = jnp.zeros(ref.shape, ref.dtype)

    source_gain = vec_ref[ROW_SOURCE : ROW_SOURCE + 1, :CIN]
    source_shift = vec_ref[ROW_SOURCE : ROW_SOURCE + 1, CIN:]

    def source_rows(rows):
        low, normed, rscale = norm_forward(
            inputs_ref[rows, :].astype(F32), source_gain, source_shift
        )
        source_ref[rows, :] = low.astype(BF16)
        hat_ref[rows, :] = normed
        rs_ref[rows, :] = rscale

    over_rows(IN_STEP, 128, source_rows)
    ao_ref[...] += dot_first(mix_ref[...], dcross_ref[...])
    add_small(ROW_COBIAS, column_sum(dcross_ref[...].astype(F32)))
    dmix_ref[...] = dot_last(dcross_ref[...], wo_ref[...]).astype(BF16)

    base = pl.multiple_of(step % (G // PER_STEP) * LAT_STEP, LAT_STEP)
    for member in range(PER_STEP):
        key_cuts, latent_cuts = group_cuts(cuts_ref, step * PER_STEP + member)
        fill_key_segments(seg_ref, key_cuts)
        dkey_ref[...] = jnp.zeros(dkey_ref.shape, F32)
        dvalue_ref[...] = jnp.zeros(dvalue_ref.shape, F32)

        def tile_back(tile, carry, member=member, key_cuts=key_cuts, latent_cuts=latent_cuts):
            row = pl.multiple_of(member * NL + tile * QT, QT)
            query_seg = query_segments(latent_cuts, tile)
            low, needed = tile_window(latent_cuts, key_cuts, IN_G, tile)

            def window(start, width):
                keys = pl.ds(member * IN_G + start, width)
                allowed = allowed_pairs(seg_ref, start, width, query_seg)
                for part in range(2):
                    query = query_ref[pl.ds(base + row, QT), half(part)]
                    key_rows = kv_ref[keys, half(part)]
                    lse = lse_ref[pl.ds((member * TILES + tile) * 2 + part, 1), :]
                    scores = dot_last(key_rows, block_diagonal(query, mask_ref[...]))
                    probs = jnp.exp2(jnp.where(allowed, scores * SCALE2 - lse, NEG_FILL))
                    dquery, dkeys, dvalues = attend_tile_back(
                        query,
                        key_rows,
                        kv_ref[keys, half(part + 2)],
                        dmix_ref[pl.ds(row, QT), half(part)],
                        probs,
                        probs.astype(BF16),
                        mask_ref[...],
                    )
                    dquery_ref[pl.ds(base + row, QT), half(part)] += dquery
                    dkey_ref[pl.ds(start, width), half(part)] += dkeys
                    dvalue_ref[pl.ds(start, width), half(part)] += dvalues

            in_windows(low, needed, IN_G, CROSS_WIDTHS, window)
            return carry

        lax.fori_loop(0, TILES, tile_back, 0)
        rows = slice(member * IN_G, member * IN_G + IN_G)
        dkv_ref[rows, :D] = (dkey_ref[...] * SCALE).astype(BF16)
        dkv_ref[rows, D:] = dvalue_ref[...].astype(BF16)

    for part in range(2):
        columns = slice(D * part, D * part + D)
        akv_ref[:, columns] += dot_first(source_ref[...], dkv_ref[:, columns])
    add_small(ROW_VBIAS, column_sum(dkv_ref[:, D:].astype(F32)))
    dinput_ref[...] = dot_last(dkv_ref[...], wkv_ref[...])

    def source_back(rows):
        dsource = dinput_ref[rows, :]
        normed = hat_ref[rows, :]
        small_ref[ROW_SOURCE : ROW_SOURCE + 1, :CIN] += column_sum(dsource * normed)
        small_ref[ROW_SOURCE : ROW_SOURCE + 1, CIN:] += column_sum(dsource)
        dinput_ref[rows, :] = norm_backward(dsource, normed, rs_ref[rows, :], source_gain)

    over_rows(IN_STEP, 128, source_back)

    @pl.when(step == last)
    def _():
        gkv_ref[...] = akv_ref[...].astype(BF16)
        go_ref[...] = ao_ref[...].astype(BF16)
        low, normed, rscale = norm_forward(
            latent_ref[...].astype(F32), vec(ROW_QGAIN), vec(ROW_QSHIFT)
        )
        dquery = (dquery_ref[...] * SCALE).astype(BF16)
        gq_ref[...] = dot_first(low.astype(BF16), dquery).astype(BF16)
        add_small(ROW_QBIAS, column_sum(dquery.astype(F32)))
        dnorm = dot_last(dquery, wq_ref[...])
        add_small(ROW_QGAIN, column_sum(dnorm * normed))
        add_small(ROW_QSHIFT, column_sum(dnorm))
        glatout_ref[...] = (
            glat_ref[...] + norm_backward(dnorm, normed, rscale, vec(ROW_QGAIN))
        ).astype(BF16)


def rows_spec(rows, columns):
    return pl.BlockSpec((rows, columns), lambda step, cuts: (step, 0))


def whole_spec(rows, columns):
    return pl.BlockSpec(
        (rows, columns), lambda step, cuts: (0, 0), pipeline_mode=pl.Buffered(1)
    )


def kernel_call(kernel, steps, in_specs, out_specs, out_shape, scratch, flops):
    return pl.pallas_call(
        kernel,
        grid_spec=pltpu.PrefetchScalarGridSpec(
            num_scalar_prefetch=1,
            grid=(steps,),
            in_specs=in_specs,
            out_specs=out_specs,
            scratch_shapes=scratch,
        ),
        out_shape=out_shape,
        compiler_params=pltpu.CompilerParams(
            vmem_limit_bytes=VMEM_BYTES, dimension_semantics=("arbitrary",)
        ),
        cost_estimate=pl.CostEstimate(
            flops=flops, bytes_accessed=100 * 2**20, transcendentals=0
        ),
    )


def gather(shard):
    return lax.all_gather(
        lax.all_gather(shard, "narrow", axis=1, tiled=True), "wide", axis=0, tiled=True
    )


def scatter(total):
    rows = lax.psum_scatter(total, "wide", scatter_dimension=0, tiled=True)
    return lax.psum_scatter(rows, "narrow", scatter_dimension=1, tiled=True).astype(F32)


def shape(rows, columns, dtype):
    return jax.ShapeDtypeStruct((rows, columns), dtype)


def local(
    inputs,
    input_segments,
    latent_segments,
    cotangent,
    latent_array,
    query_gain,
    query_shift,
    source_gain,
    source_shift,
    cross_query,
    cross_qbias,
    cross_keyval,
    cross_vbias,
    cross_output,
    cross_obias,
    self_gain,
    self_shift,
    self_project,
    self_qbias,
    self_vbias,
    self_output,
    self_obias,
    feed_gain,
    feed_shift,
    feed_upward,
    feed_ubias,
    feed_downward,
    feed_dbias,
):
    lat_rows = cotangent.shape[0]
    in_rows = inputs.shape[0]
    groups = lat_rows // NL
    steps = groups // PER_STEP

    vectors = jnp.concatenate(
        [
            query_gain,
            query_shift,
            source_gain,
            source_shift,
            cross_qbias,
            cross_vbias,
            cross_obias,
            self_gain,
            self_shift,
            self_qbias,
            self_vbias,
            self_obias,
            feed_gain,
            feed_shift,
            feed_ubias,
            feed_dbias,
            jnp.zeros(((VEC_ROWS - ROW_DBIAS - 1) * D,), BF16),
        ]
    )
    vectors = vectors.astype(F32).reshape(VEC_ROWS, D)
    marks = jnp.arange(1, SEGS, dtype=jnp.int32)
    in_cuts = jnp.sum(input_segments.reshape(groups, IN_G, 1) < marks, 1, dtype=jnp.int32)
    lat_cuts = jnp.sum(latent_segments.reshape(groups, NL, 1) < marks, 1, dtype=jnp.int32)
    blank = jnp.zeros((groups, 1), jnp.int32)
    cuts = jnp.concatenate([in_cuts, blank, lat_cuts, blank], 1)

    latent_full = gather(latent_array)
    wq = gather(cross_query)
    wkv = gather(cross_keyval)
    wo = gather(cross_output)
    wproj = gather(self_project)
    wso = gather(self_output)
    wup = gather(feed_upward)
    wdn = gather(feed_downward)

    vec_spec = whole_spec(VEC_ROWS, D)
    lse_rows = PER_STEP * TILES * 2
    after, cross_mix, keyval, lse, query = kernel_call(
        cross_forward_kernel,
        steps,
        [
            rows_spec(IN_STEP, CIN),
            whole_spec(G * NL, D),
            whole_spec(D, D),
            whole_spec(CIN, 2 * D),
            whole_spec(D, D),
            vec_spec,
        ],
        [
            rows_spec(LAT_STEP, D),
            rows_spec(LAT_STEP, D),
            rows_spec(IN_STEP, 2 * D),
            rows_spec(lse_rows, PACK),
            whole_spec(G * NL, D),
        ],
        [
            shape(lat_rows, D, F32),
            shape(lat_rows, D, BF16),
            shape(in_rows, 2 * D, BF16),
            shape(steps * lse_rows, PACK, F32),
            shape(G * NL, D, BF16),
        ],
        [
            pltpu.VMEM((IN_STEP, CIN), BF16),
            pltpu.VMEM((PACK, PACK), BF16),
            pltpu.VMEM((IN_G, 128), jnp.int32),
        ],
        60 * 10**9,
    )(cuts, inputs, latent_full, wq, wkv, wo, vectors)

    latents_out, dcross, glat, middle_small, gproj, gso, gup, gdn = kernel_call(
        middle_kernel,
        steps,
        [
            rows_spec(LAT_STEP, D),
            rows_spec(LAT_STEP, D),
            whole_spec(D, 3 * D),
            whole_spec(D, D),
            whole_spec(D, FF),
            whole_spec(FF, D),
            vec_spec,
        ],
        [
            rows_spec(LAT_STEP, D),
            rows_spec(LAT_STEP, D),
            whole_spec(G * NL, D),
            vec_spec,
            whole_spec(D, 3 * D),
            whole_spec(D, D),
            whole_spec(D, FF),
            whole_spec(FF, D),
        ],
        [
            shape(lat_rows, D, BF16),
            shape(lat_rows, D, BF16),
            shape(G * NL, D, F32),
            shape(VEC_ROWS, D, F32),
            shape(D, 3 * D, BF16),
            shape(D, D, BF16),
            shape(D, FF, BF16),
            shape(FF, D, BF16),
        ],
        [
            pltpu.VMEM((PACK, PACK), BF16),
            pltpu.VMEM((NL, 128), jnp.int32),
            pltpu.VMEM((LAT_STEP, D), F32),
            pltpu.VMEM((LAT_STEP, 1), F32),
            pltpu.VMEM((LAT_STEP, D), BF16),
            pltpu.VMEM((LAT_STEP, 3 * D), BF16),
            pltpu.VMEM((PER_STEP * TILES * 2, NL, PACK), BF16),
            pltpu.VMEM((LAT_STEP, D), BF16),
            pltpu.VMEM((LAT_STEP, D), F32),
            pltpu.VMEM((LAT_STEP, D), F32),
            pltpu.VMEM((LAT_STEP, 1), F32),
            pltpu.VMEM((LAT_STEP, D), BF16),
            pltpu.VMEM((LAT_STEP, D), F32),
            pltpu.VMEM((LAT_STEP, D), BF16),
            pltpu.VMEM((LAT_STEP, D), BF16),
            pltpu.VMEM((LAT_STEP, 3 * D), BF16),
            pltpu.VMEM((NL, D), F32),
            pltpu.VMEM((NL, D), F32),
            pltpu.VMEM((D, 3 * D), F32),
            pltpu.VMEM((D, D), F32),
            pltpu.VMEM((D, FF), F32),
            pltpu.VMEM((FF, D), F32),
        ],
        250 * 10**9,
    )(cuts, after, cotangent, wproj, wso, wup, wdn, vectors)

    dinput, glat, gq, gkv, go, cross_small = kernel_call(
        cross_backward_kernel,
        steps,
        [
            rows_spec(IN_STEP, CIN),
            rows_spec(IN_STEP, 2 * D),
            rows_spec(LAT_STEP, D),
            rows_spec(lse_rows, PACK),
            rows_spec(LAT_STEP, D),
            whole_spec(G * NL, D),
            whole_spec(G * NL, D),
            whole_spec(G * NL, D),
            whole_spec(D, D),
            whole_spec(CIN, 2 * D),
            whole_spec(D, D),
            vec_spec,
        ],
        [
            rows_spec(IN_STEP, CIN),
            whole_spec(G * NL, D),
            whole_spec(D, D),
            whole_spec(CIN, 2 * D),
            whole_spec(D, D),
            vec_spec,
        ],
        [
            shape(in_rows, CIN, F32),
            shape(G * NL, D, BF16),
            shape(D, D, BF16),
            shape(CIN, 2 * D, BF16),
            shape(D, D, BF16),
            shape(VEC_ROWS, D, F32),
        ],
        [
            pltpu.VMEM((PACK, PACK), BF16),
            pltpu.VMEM((IN_G, 128), jnp.int32),
            pltpu.VMEM((IN_STEP, CIN), BF16),
            pltpu.VMEM((IN_STEP, CIN), F32),
            pltpu.VMEM((IN_STEP, 1), F32),
            pltpu.VMEM((LAT_STEP, D), BF16),
            pltpu.VMEM((IN_G, D), F32),
            pltpu.VMEM((IN_G, D), F32),
            pltpu.VMEM((IN_STEP, 2 * D), BF16),
            pltpu.VMEM((G * NL, D), F32),
            pltpu.VMEM((CIN, 2 * D), F32),
            pltpu.VMEM((D, D), F32),
        ],
        120 * 10**9,
    )(
        cuts,
        inputs,
        keyval,
        cross_mix,
        lse,
        dcross,
        query,
        latent_full,
        glat,
        wq,
        wkv,
        wo,
        vectors,
    )

    small = lax.psum(middle_small + cross_small, ("wide", "narrow"))
    flat = small.reshape(-1)

    def part(row, size, offset=0):
        return flat[row * D + offset : row * D + offset + size]

    return (
        latents_out,
        dinput,
        scatter(glat),
        part(ROW_QGAIN, D),
        part(ROW_QSHIFT, D),
        part(ROW_SOURCE, CIN),
        part(ROW_SOURCE, CIN, CIN),
        scatter(gq),
        part(ROW_QBIAS, D),
        scatter(gkv),
        part(ROW_VBIAS, D),
        scatter(go),
        part(ROW_COBIAS, D),
        part(ROW_SGAIN, D),
        part(ROW_SSHIFT, D),
        scatter(gproj),
        part(ROW_SQBIAS, D),
        part(ROW_SVBIAS, D),
        scatter(gso),
        part(ROW_SOBIAS, D),
        part(ROW_FGAIN, D),
        part(ROW_FSHIFT, D),
        scatter(gup),
        part(ROW_UBIAS, FF),
        scatter(gdn),
        part(ROW_DBIAS, D),
    )


def solution(mesh):
    rows = P(("wide", "narrow"), None)
    flat = P(("wide", "narrow"))
    block = P("wide", "narrow")
    copied = P()
    return jax.shard_map(
        local,
        mesh=mesh,
        in_specs=(
            rows,
            flat,
            flat,
            rows,
            block,
            copied,
            copied,
            copied,
            copied,
            block,
            copied,
            block,
            copied,
            block,
            copied,
            copied,
            copied,
            block,
            copied,
            copied,
            block,
            copied,
            copied,
            copied,
            block,
            copied,
            block,
            copied,
        ),
        out_specs=(
            rows,
            rows,
            block,
            copied,
            copied,
            copied,
            copied,
            block,
            copied,
            block,
            copied,
            block,
            copied,
            copied,
            copied,
            block,
            copied,
            copied,
            block,
            copied,
            copied,
            copied,
            block,
            copied,
            block,
            copied,
        ),
        check_vma=False,
    )
```

```python
import functools

import jax
import jax.numpy as jnp
from jax import lax
from jax.experimental import pallas as pl
from jax.experimental.pallas import tpu as pltpu
from jax.sharding import PartitionSpec as P

D = 512
HEADS = 16
HD = 32
FF = 2048
CIN = 256
G = 4
NL = 256
IN_G = 512
SEGS = 4
QT = 32
PACK = 256
TILES = NL // QT
SELF_GROUPS = 2
SELF_ROWS = SELF_GROUPS * NL
CROSS_GROUPS = 4
LAT_STEP = CROSS_GROUPS * NL
IN_STEP = CROSS_GROUPS * IN_G
UNITS = 4
WIDTHS = (128, 192, 256, 384, 512)

F32 = jnp.float32
BF16 = jnp.bfloat16
NEG_FILL = -1e30
EPSILON = 1e-05
SCALE = HD**-0.5
LOG2E = 1.4426950408889634
SCALE2 = SCALE * LOG2E
VMEM_BYTES = 60 * 1024 * 1024

TAIL_RATE = 0.28
TAIL_POLY = (
    0.1165209849818009,
    0.06749547174407416,
    0.2689133347091787,
    -0.23699737809142182,
    0.38987640062523105,
    -0.10580882324798475,
)

ROW_QGAIN, ROW_QSHIFT, ROW_SOURCE, ROW_QBIAS, ROW_VBIAS, ROW_COBIAS = range(6)
ROW_SGAIN, ROW_SSHIFT, ROW_SQBIAS, ROW_SVBIAS, ROW_SOBIAS = range(6, 11)
ROW_FGAIN, ROW_FSHIFT, ROW_UBIAS, ROW_DBIAS = 11, 12, 13, 17
VEC_ROWS = 24

CHUNKS = 16
HALVES = 2
CROSS_MATS = ((G * NL, D), (D, D), (CIN, 2 * D), (D, D))
MIDDLE_MATS = ((D, 3 * D), (D, D), (D, FF), (FF, D))


def slab_place(mats, at):
    sizes = [rows // CHUNKS * (columns // (HALVES * PACK)) for rows, columns in mats]
    return sum(sizes[:at]), mats[at][0] // CHUNKS, sum(sizes)


LATENT, WQ, WKV, WO = (slab_place(CROSS_MATS, at)[:2] for at in range(4))
WPROJ, WSO, WUP, WDN = (slab_place(MIDDLE_MATS, at)[:2] for at in range(4))
CROSS_SLAB = slab_place(CROSS_MATS, 0)[2]
MIDDLE_SLAB = slab_place(MIDDLE_MATS, 0)[2]


def dot_plain(left, right):
    return lax.dot_general(left, right, (((1,), (0,)), ((), ())), preferred_element_type=F32)


def dot_first(left, right):
    return lax.dot_general(left, right, (((0,), (0,)), ((), ())), preferred_element_type=F32)


def dot_last(left, right):
    return lax.dot_general(left, right, (((1,), (1,)), ((), ())), preferred_element_type=F32)


def over_rows(total, chunk, body):
    def step(index, carry):
        body(pl.ds(pl.multiple_of(index * chunk, chunk), chunk))
        return carry

    lax.fori_loop(0, total // chunk, step, 0, unroll=8)


def norm_forward(rows, gain, shift):
    centered = rows - jnp.mean(rows, -1, keepdims=True)
    rscale = lax.rsqrt(jnp.mean(centered * centered, -1, keepdims=True) + EPSILON)
    normed = centered * rscale
    return normed * gain + shift, normed, rscale


def norm_backward(grad, normed, rscale, gain):
    dnormed = grad * gain
    return rscale * (
        dnormed
        - jnp.mean(dnormed, -1, keepdims=True)
        - normed * jnp.mean(dnormed * normed, -1, keepdims=True)
    )


def column_sum(rows):
    return jnp.sum(rows, 0, keepdims=True)


def gelu_pair(hidden):
    size = jnp.abs(hidden)
    ratio = 1.0 / (1.0 + TAIL_RATE * size)
    bell = jnp.exp2(hidden * hidden * (-0.5 * LOG2E))
    poly = TAIL_POLY[-1] * ratio
    for coefficient in TAIL_POLY[-2::-1]:
        poly = (poly + coefficient) * ratio
    tail = poly * bell
    cdf = jnp.where(hidden >= 0.0, 1.0 - tail, tail)
    return hidden * cdf, cdf + hidden * bell * 0.3989422804014327


def fill_block_mask(mask_ref):
    row_head = lax.broadcasted_iota(jnp.int32, (PACK, PACK), 0) // QT
    lane_head = lax.broadcasted_iota(jnp.int32, (PACK, PACK), 1) // HD
    mask_ref[...] = jnp.where(row_head == lane_head, 1.0, 0.0).astype(BF16)


def block_diagonal(rows, mask):
    return jnp.concatenate([rows] * (PACK // QT), 0) * mask


def take_diagonal(full):
    lane = lax.broadcasted_iota(jnp.int32, (QT, 128), 1)
    columns = []
    for half in range(2):
        base = 128 * half
        picked = full[base : base + QT, base : base + 128]
        for head in range(1, 4):
            row = base + QT * head
            picked = jnp.where(
                lane >= HD * head, full[row : row + QT, base : base + 128], picked
            )
        columns.append(picked)
    return jnp.concatenate(columns, 1)


def segment_at(cuts, place):
    return sum((place >= cut).astype(jnp.int32) for cut in cuts)


def pick(index, values):
    result = values[0]
    for at in range(1, len(values)):
        result = jnp.where(index == at, values[at], result)
    return result


def in_widths(needed, body):
    smaller = 0
    for width in WIDTHS:

        @pl.when((needed > smaller) & (needed <= width))
        def _(width=width):
            body(width)

        smaller = width


def query_segments(query_cuts, tile):
    lane = lax.broadcasted_iota(jnp.int32, (1, PACK), 1) % QT
    return segment_at(query_cuts, tile * QT + lane)


def allowed_pairs(key_seg, query_seg):
    return jnp.concatenate([key_seg, key_seg], 1) == query_seg


def softmax_rows(scores, allowed):
    scores = jnp.where(allowed, scores, NEG_FILL)
    top = jnp.max(scores, 0, keepdims=True)
    powers = jnp.exp2((scores - top) * SCALE2)
    total = jnp.sum(powers, 0, keepdims=True)
    return (powers * (1.0 / total)).astype(BF16), top * SCALE2 + jnp.log2(total)


def score_grads(probs, dprobs):
    weighted = probs * dprobs
    delta = jnp.sum(weighted, 0, keepdims=True)
    return (weighted - probs * delta).astype(BF16)


def half(part):
    return slice(PACK * part, PACK * part + PACK)


def slab_part(slab_ref, place, side, piece):
    offset, rows = place
    part = slab_ref[:, side, offset + piece * rows : offset + piece * rows + rows, :]
    return part.reshape(CHUNKS * rows, PACK)


def slab_matrix(slab_ref, place, pieces):
    return jnp.concatenate(
        [
            slab_part(slab_ref, place, piece // (pieces // HALVES), piece % (pieces // HALVES))
            for piece in range(pieces)
        ],
        1,
    )


def store_slab(slab_ref, place, matrix):
    offset, rows = place
    pieces = matrix.shape[1] // PACK
    for piece in range(pieces):
        side, inner = piece // (pieces // HALVES), piece % (pieces // HALVES)
        start = offset + inner * rows
        part = matrix[:, piece * PACK : piece * PACK + PACK].astype(BF16)
        slab_ref[:, side, start : start + rows, :] = part.reshape(CHUNKS, rows, PACK)


def latent_cuts(cuts_ref, group):
    return [cuts_ref[group, 4 + at] for at in range(SEGS - 1)]


def fill_cross_segments(seg_ref, cuts_ref, step):
    place = lax.broadcasted_iota(jnp.int32, (IN_G, 128), 0)
    for member in range(CROSS_GROUPS):
        key_cuts = [cuts_ref[step * CROSS_GROUPS + member, at] for at in range(SEGS - 1)]
        seg_ref[member * IN_G : member * IN_G + IN_G, :] = segment_at(key_cuts, place)


def cross_units(plan_ref, cuts_ref, seg_ref, step, batch, width):
    units = []
    for at in range(UNITS):
        packed = plan_ref[step, batch * UNITS + at]
        slot = packed // 1024
        start = pl.multiple_of(jnp.minimum(packed % 1024, IN_G - width), 16)
        member = slot // TILES
        tile = slot % TILES
        keys = pl.ds(pl.multiple_of(member * IN_G + start, 16), width)
        cuts = latent_cuts(cuts_ref, step * CROSS_GROUPS + member)
        allowed = allowed_pairs(seg_ref[keys, :], query_segments(cuts, tile))
        units.append((slot, pl.ds(pl.multiple_of(slot * QT, QT), QT), keys, allowed))
    return units


def batch_needed(plan_ref, step, batch):
    return plan_ref[step, CROSS_GROUPS * TILES + batch]


def plan_tiles(in_cuts, lat_cuts):
    groups = in_cuts.shape[0]
    tile = jnp.arange(TILES, dtype=jnp.int32) * QT
    first = jnp.sum(tile[None, :, None] >= lat_cuts[:, None, :], -1, dtype=jnp.int32)
    last = jnp.sum(tile[None, :, None] + (QT - 1) >= lat_cuts[:, None, :], -1, dtype=jnp.int32)
    starts = jnp.concatenate([jnp.zeros((groups, 1), jnp.int32), in_cuts], 1)
    ends = jnp.concatenate([in_cuts, jnp.full((groups, 1), IN_G, jnp.int32)], 1)
    segment = jnp.arange(SEGS, dtype=jnp.int32)
    low = jnp.sum(jnp.where(first[..., None] == segment, starts[:, None, :], 0), -1) // 16 * 16
    high = jnp.sum(jnp.where(last[..., None] == segment, ends[:, None, :], 0), -1)
    count = CROSS_GROUPS * TILES
    low = low.reshape(-1, count)
    needed = high.reshape(-1, count) - low
    slot = jnp.arange(count, dtype=jnp.int32)
    earlier = slot[:, None] < slot[None, :]
    mine, other = needed[:, None, :], needed[:, :, None]
    rank = jnp.sum((other < mine) | ((other == mine) & earlier), 1, dtype=jnp.int32)
    place = rank[:, None, :] == slot[:, None]
    packed = jnp.sum(jnp.where(place, (slot * 1024 + low)[:, None, :], 0), -1)
    batches = jnp.arange(count // UNITS, dtype=jnp.int32)[:, None]
    inside = rank[:, None, :] // UNITS == batches
    widest = jnp.max(jnp.where(inside, needed[:, None, :], 0), -1)
    return jnp.concatenate([packed, widest], 1).astype(jnp.int32)


def cross_forward_kernel(
    cuts_ref,
    plan_ref,
    source_ref,
    slab_ref,
    vec_ref,
    after_ref,
    mix_ref,
    kv_ref,
    lse_ref,
    query_ref,
    mask_ref,
    seg_ref,
):
    step = pl.program_id(0)

    @pl.when(step == 0)
    def _():
        fill_block_mask(mask_ref)
        low, _, _ = norm_forward(
            slab_matrix(slab_ref, LATENT, 2).astype(F32),
            vec_ref[ROW_QGAIN : ROW_QGAIN + 1, :],
            vec_ref[ROW_QSHIFT : ROW_QSHIFT + 1, :],
        )
        query = dot_plain(low.astype(BF16), slab_matrix(slab_ref, WQ, 2))
        query_ref[...] = (query + vec_ref[ROW_QBIAS : ROW_QBIAS + 1, :]).astype(BF16)

    wkv = slab_matrix(slab_ref, WKV, 4)
    kv_ref[:, :D] = dot_plain(source_ref[...], wkv[:, :D]).astype(BF16)
    kv_ref[:, D:] = (
        dot_plain(source_ref[...], wkv[:, D:]) + vec_ref[ROW_VBIAS : ROW_VBIAS + 1, :]
    ).astype(BF16)

    fill_cross_segments(seg_ref, cuts_ref, step)

    def batch_body(batch, carry):
        def window(width):
            units = cross_units(plan_ref, cuts_ref, seg_ref, step, batch, width)
            scores = [
                dot_last(
                    kv_ref[keys, half(part)],
                    block_diagonal(query_ref[rows, half(part)], mask_ref[...]),
                )
                for _, rows, keys, _ in units
                for part in range(2)
            ]
            probs = []
            for at, (slot, _, _, allowed) in enumerate(units):
                for part in range(2):
                    low, lse = softmax_rows(scores[2 * at + part], allowed)
                    probs.append(low)
                    lse_ref[pl.ds(slot * 2 + part, 1), :] = lse
            for at, (_, rows, keys, _) in enumerate(units):
                for part in range(2):
                    full = dot_first(probs[2 * at + part], kv_ref[keys, half(part + 2)])
                    mix_ref[rows, half(part)] = take_diagonal(full).astype(BF16)

        in_widths(batch_needed(plan_ref, step, batch), window)
        return carry

    lax.fori_loop(0, CROSS_GROUPS * TILES // UNITS, batch_body, 0)
    after_ref[...] = (
        slab_matrix(slab_ref, LATENT, 2).astype(F32)
        + dot_plain(mix_ref[...], slab_matrix(slab_ref, WO, 2))
        + vec_ref[ROW_COBIAS : ROW_COBIAS + 1, :]
    )


def middle_kernel(
    cuts_ref,
    after_ref,
    cot_ref,
    slab_ref,
    vec_ref,
    out_ref,
    dcross_ref,
    glat_ref,
    small_ref,
    gslab_ref,
    mask_ref,
    hat1_ref,
    rs1_ref,
    low1_ref,
    triple_ref,
    probs_ref,
    mix_ref,
    res_ref,
    hat2_ref,
    rs2_ref,
    low2_ref,
    dtop_ref,
    dso_ref,
    dmix_ref,
    dtriple_ref,
    aproj_ref,
    aso_ref,
    aup_ref,
    adn_ref,
):
    step = pl.program_id(0)
    last = pl.num_programs(0) - 1

    def vec(row):
        return vec_ref[row : row + 1, :]

    def add_small(row, value):
        small_ref[row : row + 1, :] += value

    @pl.when(step == 0)
    def _():
        fill_block_mask(mask_ref)
        for ref in (glat_ref, small_ref, aproj_ref, aso_ref, aup_ref, adn_ref):
            ref[...] = jnp.zeros(ref.shape, ref.dtype)

    def first_norm(rows):
        low, normed, rscale = norm_forward(after_ref[rows, :], vec(ROW_SGAIN), vec(ROW_SSHIFT))
        low1_ref[rows, :] = low.astype(BF16)
        hat1_ref[rows, :] = normed
        rs1_ref[rows, :] = rscale

    over_rows(SELF_ROWS, 64, first_norm)
    wproj = slab_matrix(slab_ref, WPROJ, 6)
    for block, bias in enumerate((ROW_SQBIAS, None, ROW_SVBIAS)):
        columns = slice(D * block, D * block + D)
        product = dot_plain(low1_ref[...], wproj[:, columns])
        if bias is not None:
            product = product + vec(bias)
        triple_ref[:, columns] = product.astype(BF16)

    def attend_group(member, carry):
        start = pl.multiple_of(member * NL, NL)
        group = pl.ds(start, NL)
        cuts = latent_cuts(cuts_ref, step * SELF_GROUPS + member)
        key_seg = segment_at(cuts, lax.broadcasted_iota(jnp.int32, (NL, 128), 0))
        tiles = [pl.ds(pl.multiple_of(start + tile * QT, QT), QT) for tile in range(TILES)]
        scores = [
            dot_last(
                triple_ref[group, half(part + 2)],
                block_diagonal(triple_ref[rows, half(part)], mask_ref[...]),
            )
            for rows in tiles
            for part in range(2)
        ]
        probs = []
        for tile in range(TILES):
            allowed = allowed_pairs(key_seg, query_segments(cuts, tile))
            for part in range(2):
                low, _ = softmax_rows(scores[2 * tile + part], allowed)
                probs.append(low)
                probs_ref[(member * TILES + tile) * 2 + part] = low
        for tile, rows in enumerate(tiles):
            for part in range(2):
                full = dot_first(probs[2 * tile + part], triple_ref[group, half(part + 4)])
                mix_ref[rows, half(part)] = take_diagonal(full).astype(BF16)
        return carry

    lax.fori_loop(0, SELF_GROUPS, attend_group, 0)

    res_ref[...] = after_ref[...] + dot_plain(mix_ref[...], slab_matrix(slab_ref, WSO, 2)) + vec(ROW_SOBIAS)

    def second_norm(rows):
        low, normed, rscale = norm_forward(res_ref[rows, :], vec(ROW_FGAIN), vec(ROW_FSHIFT))
        low2_ref[rows, :] = low.astype(BF16)
        hat2_ref[rows, :] = normed
        rs2_ref[rows, :] = rscale

    over_rows(SELF_ROWS, 64, second_norm)
    dtop_ref[...] = jnp.zeros(dtop_ref.shape, F32)

    def feed_block(block, carry):
        columns = pl.ds(pl.multiple_of(block * D, D), D)
        offset, height = WUP
        side = block // 2
        wup = jnp.concatenate(
            [
                slab_ref[
                    :,
                    side,
                    pl.ds(pl.multiple_of(offset + (block % 2 * 2 + piece) * height, height), height),
                    :,
                ].reshape(D, PACK)
                for piece in range(2)
            ],
            1,
        )
        offset, height = WDN
        chunks = pl.ds(block * (D // height), D // height)
        wdn = jnp.concatenate(
            [
                slab_ref[chunks, piece, offset : offset + height, :].reshape(D, PACK)
                for piece in range(2)
            ],
            1,
        )
        hidden = dot_plain(low2_ref[...], wup) + vec_ref[pl.ds(ROW_UBIAS + block, 1), :]
        active, slope = gelu_pair(hidden)
        active = active.astype(BF16)
        dhidden = (slope * dot_last(cot_ref[...], wdn)).astype(BF16)
        small_ref[pl.ds(ROW_UBIAS + block, 1), :] += column_sum(dhidden.astype(F32))
        res_ref[...] += dot_plain(active, wdn)
        adn_ref[columns, :] += dot_first(active, cot_ref[...])
        aup_ref[:, columns] += dot_first(low2_ref[...], dhidden)
        dtop_ref[...] += dot_last(dhidden, wup)
        return carry

    lax.fori_loop(0, FF // D, feed_block, 0)

    def after_feed(rows):
        out_ref[rows, :] = (res_ref[rows, :] + vec(ROW_DBIAS)).astype(BF16)
        dtop = dtop_ref[rows, :]
        normed = hat2_ref[rows, :]
        cot = cot_ref[rows, :].astype(F32)
        dafter = cot + norm_backward(dtop, normed, rs2_ref[rows, :], vec(ROW_FGAIN))
        dlow = dafter.astype(BF16)
        res_ref[rows, :] = dafter
        dso_ref[rows, :] = dlow
        add_small(ROW_FGAIN, column_sum(dtop * normed))
        add_small(ROW_FSHIFT, column_sum(dtop))
        add_small(ROW_DBIAS, column_sum(cot))
        add_small(ROW_SOBIAS, column_sum(dlow.astype(F32)))

    over_rows(SELF_ROWS, 64, after_feed)
    aso_ref[...] += dot_first(mix_ref[...], dso_ref[...])
    dmix_ref[...] = dot_last(dso_ref[...], slab_matrix(slab_ref, WSO, 2)).astype(BF16)

    def attend_group_back(member, carry):
        start = pl.multiple_of(member * NL, NL)
        group = pl.ds(start, NL)
        tiles = [pl.ds(pl.multiple_of(start + tile * QT, QT), QT) for tile in range(TILES)]
        for part in range(2):
            keys = triple_ref[group, half(part + 2)]
            values = triple_ref[group, half(part + 4)]
            queries = [block_diagonal(triple_ref[rows, half(part)], mask_ref[...]) for rows in tiles]
            grads = [block_diagonal(dmix_ref[rows, half(part)], mask_ref[...]) for rows in tiles]
            dprobs = [dot_last(values, grad) for grad in grads]
            probs = [probs_ref[(member * TILES + tile) * 2 + part] for tile in range(TILES)]
            dscores = [score_grads(low.astype(F32), dp) for low, dp in zip(probs, dprobs)]
            dvalues = dot_plain(jnp.concatenate(probs, 1), jnp.concatenate(grads, 0))
            dtriple_ref[group, half(part + 4)] = dvalues.astype(BF16)
            dkeys = dot_plain(jnp.concatenate(dscores, 1), jnp.concatenate(queries, 0))
            dtriple_ref[group, half(part + 2)] = (dkeys * SCALE).astype(BF16)
            for rows, dscore in zip(tiles, dscores):
                dquery = take_diagonal(dot_first(dscore, keys))
                dtriple_ref[rows, half(part)] = (dquery * SCALE).astype(BF16)
        return carry

    lax.fori_loop(0, SELF_GROUPS, attend_group_back, 0)
    for block in range(3):
        columns = slice(D * block, D * block + D)
        aproj_ref[:, columns] += dot_first(low1_ref[...], dtriple_ref[:, columns])
    add_small(ROW_SQBIAS, column_sum(dtriple_ref[:, :D].astype(F32)))
    add_small(ROW_SVBIAS, column_sum(dtriple_ref[:, 2 * D :].astype(F32)))
    dtop_ref[...] = dot_last(dtriple_ref[...], slab_matrix(slab_ref, WPROJ, 6))
    base = step % (G // SELF_GROUPS) * SELF_ROWS

    def after_self(rows):
        dmid = dtop_ref[rows, :]
        normed = hat1_ref[rows, :]
        dafter = res_ref[rows, :] + norm_backward(dmid, normed, rs1_ref[rows, :], vec(ROW_SGAIN))
        dcross_ref[rows, :] = dafter.astype(BF16)
        glat_ref[pl.ds(pl.multiple_of(base + rows.start, 64), rows.size), :] += dafter
        add_small(ROW_SGAIN, column_sum(dmid * normed))
        add_small(ROW_SSHIFT, column_sum(dmid))

    over_rows(SELF_ROWS, 64, after_self)

    @pl.when(step == last)
    def _():
        store_slab(gslab_ref, WPROJ, aproj_ref[...])
        store_slab(gslab_ref, WSO, aso_ref[...])
        store_slab(gslab_ref, WUP, aup_ref[...])
        store_slab(gslab_ref, WDN, adn_ref[...])


def cross_backward_kernel(
    cuts_ref,
    plan_ref,
    inputs_ref,
    kv_ref,
    mix_ref,
    lse_ref,
    dcross_ref,
    query_ref,
    glat_ref,
    slab_ref,
    vec_ref,
    dinput_ref,
    gslab_ref,
    small_ref,
    mask_ref,
    seg_ref,
    source_ref,
    rs_ref,
    dmix_ref,
    dkey_ref,
    dvalue_ref,
    dkv_ref,
    dquery_ref,
    akv_ref,
    ao_ref,
):
    step = pl.program_id(0)
    last = pl.num_programs(0) - 1

    def vec(row):
        return vec_ref[row : row + 1, :]

    def add_small(row, value):
        small_ref[row : row + 1, :] += value

    @pl.when(step == 0)
    def _():
        fill_block_mask(mask_ref)
        for ref in (small_ref, dquery_ref, akv_ref, ao_ref):
            ref[...] = jnp.zeros(ref.shape, ref.dtype)

    source_gain = vec_ref[ROW_SOURCE : ROW_SOURCE + 1, :CIN]
    source_shift = vec_ref[ROW_SOURCE : ROW_SOURCE + 1, CIN:]

    def source_rows(rows):
        low, normed, rscale = norm_forward(
            inputs_ref[rows, :].astype(F32), source_gain, source_shift
        )
        source_ref[rows, :] = low.astype(BF16)
        dinput_ref[rows, :] = normed
        rs_ref[rows, :] = rscale

    over_rows(IN_STEP, 128, source_rows)
    ao_ref[...] += dot_first(mix_ref[...], dcross_ref[...])
    add_small(ROW_COBIAS, column_sum(dcross_ref[...].astype(F32)))
    dmix_ref[...] = dot_last(dcross_ref[...], slab_matrix(slab_ref, WO, 2)).astype(BF16)

    fill_cross_segments(seg_ref, cuts_ref, step)
    dkey_ref[...] = jnp.zeros(dkey_ref.shape, F32)
    dvalue_ref[...] = jnp.zeros(dvalue_ref.shape, F32)

    def batch_body(batch, carry):
        def window(width):
            units = cross_units(plan_ref, cuts_ref, seg_ref, step, batch, width)
            work = []
            for slot, rows, keys, allowed in units:
                for part in range(2):
                    queries = block_diagonal(query_ref[rows, half(part)], mask_ref[...])
                    grads = block_diagonal(dmix_ref[rows, half(part)], mask_ref[...])
                    scores = dot_last(kv_ref[keys, half(part)], queries)
                    dprobs = dot_last(kv_ref[keys, half(part + 2)], grads)
                    work.append((slot, rows, keys, allowed, part, queries, grads, scores, dprobs))
            ready = []
            for slot, rows, keys, allowed, part, queries, grads, scores, dprobs in work:
                lse = lse_ref[pl.ds(slot * 2 + part, 1), :]
                probs = jnp.exp2(jnp.where(allowed, scores * SCALE2 - lse, NEG_FILL))
                dscores = score_grads(probs, dprobs)
                ready.append((rows, keys, part, queries, grads, probs.astype(BF16), dscores))
            for rows, keys, part, queries, grads, probs, dscores in ready:
                dvalue_ref[keys, half(part)] += dot_plain(probs, grads)
                dkey_ref[keys, half(part)] += dot_plain(dscores, queries)
                dquery_ref[rows, half(part)] += take_diagonal(
                    dot_first(dscores, kv_ref[keys, half(part)])
                )

        in_widths(batch_needed(plan_ref, step, batch), window)
        return carry

    lax.fori_loop(0, CROSS_GROUPS * TILES // UNITS, batch_body, 0)
    dkv_ref[:, :D] = (dkey_ref[...] * SCALE).astype(BF16)
    dkv_ref[:, D:] = dvalue_ref[...].astype(BF16)

    for part in range(2):
        columns = slice(D * part, D * part + D)
        akv_ref[:, columns] += dot_first(source_ref[...], dkv_ref[:, columns])
    add_small(ROW_VBIAS, column_sum(dkv_ref[:, D:].astype(F32)))

    def source_back(rows):
        dsource = dot_last(dkv_ref[rows, :], slab_matrix(slab_ref, WKV, 4))
        normed = dinput_ref[rows, :]
        small_ref[ROW_SOURCE : ROW_SOURCE + 1, :CIN] += column_sum(dsource * normed)
        small_ref[ROW_SOURCE : ROW_SOURCE + 1, CIN:] += column_sum(dsource)
        dinput_ref[rows, :] = norm_backward(dsource, normed, rs_ref[rows, :], source_gain)

    over_rows(IN_STEP, 256, source_back)

    @pl.when(step == last)
    def _():
        store_slab(gslab_ref, WKV, akv_ref[...])
        store_slab(gslab_ref, WO, ao_ref[...])
        low, normed, rscale = norm_forward(
            slab_matrix(slab_ref, LATENT, 2).astype(F32), vec(ROW_QGAIN), vec(ROW_QSHIFT)
        )
        dquery = (dquery_ref[...] * SCALE).astype(BF16)
        store_slab(gslab_ref, WQ, dot_first(low.astype(BF16), dquery))
        add_small(ROW_QBIAS, column_sum(dquery.astype(F32)))
        dnorm = dot_last(dquery, slab_matrix(slab_ref, WQ, 2))
        add_small(ROW_QGAIN, column_sum(dnorm * normed))
        add_small(ROW_QSHIFT, column_sum(dnorm))
        total = glat_ref[...] + norm_backward(dnorm, normed, rscale, vec(ROW_QGAIN))
        store_slab(gslab_ref, LATENT, total)


def rows_spec(rows, columns):
    return pl.BlockSpec((rows, columns), lambda step, *scalars: (step, 0))


def whole_spec(rows, columns):
    return pl.BlockSpec(
        (rows, columns), lambda step, *scalars: (0, 0), pipeline_mode=pl.Buffered(1)
    )


def kernel_call(kernel, scalars, steps, in_specs, out_specs, out_shape, scratch, flops):
    return pl.pallas_call(
        kernel,
        grid_spec=pltpu.PrefetchScalarGridSpec(
            num_scalar_prefetch=scalars,
            grid=(steps,),
            in_specs=in_specs,
            out_specs=out_specs,
            scratch_shapes=scratch,
        ),
        out_shape=out_shape,
        compiler_params=pltpu.CompilerParams(
            vmem_limit_bytes=VMEM_BYTES, dimension_semantics=("arbitrary",)
        ),
        cost_estimate=pl.CostEstimate(
            flops=flops, bytes_accessed=100 * 2**20, transcendentals=0
        ),
    )


def slab_spec(rows):
    return pl.BlockSpec(
        (CHUNKS, HALVES, rows, PACK),
        lambda step, *scalars: (0, 0, 0, 0),
        pipeline_mode=pl.Buffered(1),
    )


def slab_shape(rows):
    return jax.ShapeDtypeStruct((CHUNKS, HALVES, rows, PACK), BF16)


def pack_shards(shards):
    return jnp.concatenate(
        [
            shard[:, start : start + PACK]
            for shard in shards
            for start in range(0, shard.shape[1], PACK)
        ],
        0,
    )


def unpack_shards(packed, mats):
    shards = []
    start = 0
    for rows, columns in mats:
        height = rows // CHUNKS
        pieces = []
        for _ in range(columns // (HALVES * PACK)):
            pieces.append(packed[start : start + height])
            start += height
        shards.append(jnp.concatenate(pieces, 1))
    return shards


def gather_whole(shards):
    parts = []
    for shard in shards:
        full = lax.all_gather(
            lax.all_gather(shard, "narrow", axis=1, tiled=True), "wide", axis=0, tiled=True
        )
        rows, columns = full.shape
        split = full.reshape(CHUNKS, rows // CHUNKS, HALVES, columns // (HALVES * PACK), PACK)
        parts.append(split.transpose(0, 2, 3, 1, 4).reshape(CHUNKS, HALVES, -1, PACK))
    return jnp.concatenate(parts, 2)


def scatter_whole(slab, mats):
    shards = []
    start = 0
    for rows, columns in mats:
        height = rows // CHUNKS
        pieces = columns // (HALVES * PACK)
        part = slab[:, :, start : start + height * pieces]
        start += height * pieces
        part = part.reshape(CHUNKS, HALVES, pieces, height, PACK).transpose(0, 3, 1, 2, 4)
        total = lax.psum_scatter(
            part.reshape(rows, columns), "wide", scatter_dimension=0, tiled=True
        )
        total = lax.psum_scatter(total, "narrow", scatter_dimension=1, tiled=True)
        shards.append(total.astype(F32))
    return shards


SWAP = ((0, 1), (1, 0))


def gather_soon(shards):
    packed = pack_shards(shards)
    copies = jnp.broadcast_to(packed, (CHUNKS,) + packed.shape)
    mine = lax.all_to_all(copies, "wide", 0, 0)
    other = lax.ppermute(mine, "narrow", SWAP)
    first = lax.axis_index("narrow") == 0
    return jnp.stack([jnp.where(first, mine, other), jnp.where(first, other, mine)], 1)


def gather_later(shards):
    packed = pack_shards(shards)
    full = lax.all_gather(packed, ("wide", "narrow"), axis=0)
    return full.reshape((CHUNKS, HALVES) + packed.shape)


def sum_halves(slab):
    first = lax.axis_index("narrow") == 0
    sent = lax.ppermute(jnp.where(first, slab[:, 1], slab[:, 0]), "narrow", SWAP)
    kept = jnp.where(first, slab[:, 0], slab[:, 1])
    return (sent.astype(F32) + kept.astype(F32)).astype(BF16)


def scatter_soon(slab, mats):
    parts = lax.all_to_all(sum_halves(slab), "wide", 0, 0)
    return unpack_shards(jnp.sum(parts.astype(F32), 0), mats)


def sum_small_soon(rows):
    pair = rows + lax.ppermute(rows, "narrow", SWAP)
    copies = jnp.broadcast_to(pair, (CHUNKS,) + pair.shape)
    return jnp.sum(lax.all_to_all(copies, "wide", 0, 0), 0)


def scatter_later(slab, mats):
    total = lax.psum_scatter(sum_halves(slab), "wide", scatter_dimension=0)
    return unpack_shards(total.astype(F32), mats)


def shape(rows, columns, dtype):
    return jax.ShapeDtypeStruct((rows, columns), dtype)


def local(
    wide,
    narrow,
    inputs,
    input_segments,
    latent_segments,
    cotangent,
    latent_array,
    query_gain,
    query_shift,
    source_gain,
    source_shift,
    cross_query,
    cross_qbias,
    cross_keyval,
    cross_vbias,
    cross_output,
    cross_obias,
    self_gain,
    self_shift,
    self_project,
    self_qbias,
    self_vbias,
    self_output,
    self_obias,
    feed_gain,
    feed_shift,
    feed_upward,
    feed_ubias,
    feed_downward,
    feed_dbias,
):
    lat_rows = cotangent.shape[0]
    in_rows = inputs.shape[0]
    groups = lat_rows // NL
    steps = groups // CROSS_GROUPS
    self_steps = groups // SELF_GROUPS

    vectors = jnp.concatenate(
        [
            query_gain,
            query_shift,
            source_gain,
            source_shift,
            cross_qbias,
            cross_vbias,
            cross_obias,
            self_gain,
            self_shift,
            self_qbias,
            self_vbias,
            self_obias,
            feed_gain,
            feed_shift,
            feed_ubias,
            feed_dbias,
            jnp.zeros(((VEC_ROWS - ROW_DBIAS - 1) * D,), BF16),
        ]
    )
    vectors = vectors.astype(F32).reshape(VEC_ROWS, D)
    marks = jnp.arange(1, SEGS, dtype=jnp.int32)
    in_cuts = jnp.sum(input_segments.reshape(groups, IN_G, 1) < marks, 1, dtype=jnp.int32)
    lat_cuts = jnp.sum(latent_segments.reshape(groups, NL, 1) < marks, 1, dtype=jnp.int32)
    blank = jnp.zeros((groups, 1), jnp.int32)
    cuts = jnp.concatenate([in_cuts, blank, lat_cuts, blank], 1)
    plan = plan_tiles(in_cuts, lat_cuts)

    source_low, _, _ = norm_forward(
        inputs.astype(F32), source_gain.astype(F32), source_shift.astype(F32)
    )
    source_low = source_low.astype(BF16)

    cross_shards = (latent_array, cross_query, cross_keyval, cross_output)
    middle_shards = (self_project, self_output, feed_upward, feed_downward)
    packed = (wide, narrow) == (CHUNKS, HALVES)
    if packed:
        cross_slab = gather_soon(cross_shards)
        middle_slab = gather_later(middle_shards)
    else:
        cross_slab = gather_whole(cross_shards)
        middle_slab = gather_whole(middle_shards)

    vec_spec = whole_spec(VEC_ROWS, D)
    lse_rows = CROSS_GROUPS * TILES * 2
    after, cross_mix, keyval, lse, query = kernel_call(
        cross_forward_kernel,
        2,
        steps,
        [
            rows_spec(IN_STEP, CIN),
            slab_spec(CROSS_SLAB),
            vec_spec,
        ],
        [
            rows_spec(LAT_STEP, D),
            rows_spec(LAT_STEP, D),
            rows_spec(IN_STEP, 2 * D),
            rows_spec(lse_rows, PACK),
            whole_spec(G * NL, D),
        ],
        [
            shape(lat_rows, D, F32),
            shape(lat_rows, D, BF16),
            shape(in_rows, 2 * D, BF16),
            shape(steps * lse_rows, PACK, F32),
            shape(G * NL, D, BF16),
        ],
        [
            pltpu.VMEM((PACK, PACK), BF16),
            pltpu.VMEM((IN_STEP, 128), jnp.int32),
        ],
        60 * 10**9,
    )(cuts, plan, source_low, cross_slab, vectors)

    latents_out, dcross, glat, middle_small, middle_grads = kernel_call(
        middle_kernel,
        1,
        self_steps,
        [
            rows_spec(SELF_ROWS, D),
            rows_spec(SELF_ROWS, D),
            slab_spec(MIDDLE_SLAB),
            vec_spec,
        ],
        [
            rows_spec(SELF_ROWS, D),
            rows_spec(SELF_ROWS, D),
            whole_spec(G * NL, D),
            vec_spec,
            slab_spec(MIDDLE_SLAB),
        ],
        [
            shape(lat_rows, D, BF16),
            shape(lat_rows, D, BF16),
            shape(G * NL, D, F32),
            shape(VEC_ROWS, D, F32),
            slab_shape(MIDDLE_SLAB),
        ],
        [
            pltpu.VMEM((PACK, PACK), BF16),
            pltpu.VMEM((SELF_ROWS, D), F32),
            pltpu.VMEM((SELF_ROWS, 1), F32),
            pltpu.VMEM((SELF_ROWS, D), BF16),
            pltpu.VMEM((SELF_ROWS, 3 * D), BF16),
            pltpu.VMEM((SELF_GROUPS * TILES * 2, NL, PACK), BF16),
            pltpu.VMEM((SELF_ROWS, D), BF16),
            pltpu.VMEM((SELF_ROWS, D), F32),
            pltpu.VMEM((SELF_ROWS, D), F32),
            pltpu.VMEM((SELF_ROWS, 1), F32),
            pltpu.VMEM((SELF_ROWS, D), BF16),
            pltpu.VMEM((SELF_ROWS, D), F32),
            pltpu.VMEM((SELF_ROWS, D), BF16),
            pltpu.VMEM((SELF_ROWS, D), BF16),
            pltpu.VMEM((SELF_ROWS, 3 * D), BF16),
            pltpu.VMEM((D, 3 * D), F32),
            pltpu.VMEM((D, D), F32),
            pltpu.VMEM((D, FF), F32),
            pltpu.VMEM((FF, D), F32),
        ],
        250 * 10**9,
    )(cuts, after, cotangent, middle_slab, vectors)

    dinput, cross_grads, cross_small = kernel_call(
        cross_backward_kernel,
        2,
        steps,
        [
            rows_spec(IN_STEP, CIN),
            rows_spec(IN_STEP, 2 * D),
            rows_spec(LAT_STEP, D),
            rows_spec(lse_rows, PACK),
            rows_spec(LAT_STEP, D),
            whole_spec(G * NL, D),
            whole_spec(G * NL, D),
            slab_spec(CROSS_SLAB),
            vec_spec,
        ],
        [
            rows_spec(IN_STEP, CIN),
            slab_spec(CROSS_SLAB),
            vec_spec,
        ],
        [
            shape(in_rows, CIN, F32),
            slab_shape(CROSS_SLAB),
            shape(VEC_ROWS, D, F32),
        ],
        [
            pltpu.VMEM((PACK, PACK), BF16),
            pltpu.VMEM((IN_STEP, 128), jnp.int32),
            pltpu.VMEM((IN_STEP, CIN), BF16),
            pltpu.VMEM((IN_STEP, 1), F32),
            pltpu.VMEM((LAT_STEP, D), BF16),
            pltpu.VMEM((IN_STEP, D), F32),
            pltpu.VMEM((IN_STEP, D), F32),
            pltpu.VMEM((IN_STEP, 2 * D), BF16),
            pltpu.VMEM((G * NL, D), F32),
            pltpu.VMEM((CIN, 2 * D), F32),
            pltpu.VMEM((D, D), F32),
        ],
        120 * 10**9,
    )(
        cuts,
        plan,
        inputs,
        keyval,
        cross_mix,
        lse,
        dcross,
        query,
        glat,
        cross_slab,
        vectors,
    )

    axes = ("wide", "narrow")
    middle_sum = lax.psum(middle_small, axes)[ROW_SGAIN:]
    if packed:
        gproj, gso, gup, gdn = scatter_later(middle_grads, MIDDLE_MATS)
        cross_sum = sum_small_soon(cross_small[:8])
        glatent, gq, gkv, go = scatter_soon(cross_grads, CROSS_MATS)
    else:
        gproj, gso, gup, gdn = scatter_whole(middle_grads, MIDDLE_MATS)
        cross_sum = lax.psum(cross_small, axes)
        glatent, gq, gkv, go = scatter_whole(cross_grads, CROSS_MATS)
    flat = jnp.concatenate([cross_sum[:ROW_SGAIN].reshape(-1), middle_sum.reshape(-1)])

    def part(row, size, offset=0):
        return flat[row * D + offset : row * D + offset + size]

    return (
        latents_out,
        dinput,
        glatent,
        part(ROW_QGAIN, D),
        part(ROW_QSHIFT, D),
        part(ROW_SOURCE, CIN),
        part(ROW_SOURCE, CIN, CIN),
        gq,
        part(ROW_QBIAS, D),
        gkv,
        part(ROW_VBIAS, D),
        go,
        part(ROW_COBIAS, D),
        part(ROW_SGAIN, D),
        part(ROW_SSHIFT, D),
        gproj,
        part(ROW_SQBIAS, D),
        part(ROW_SVBIAS, D),
        gso,
        part(ROW_SOBIAS, D),
        part(ROW_FGAIN, D),
        part(ROW_FSHIFT, D),
        gup,
        part(ROW_UBIAS, FF),
        gdn,
        part(ROW_DBIAS, D),
    )


def solution(mesh):
    rows = P(("wide", "narrow"), None)
    flat = P(("wide", "narrow"))
    block = P("wide", "narrow")
    copied = P()
    return jax.shard_map(
        functools.partial(local, mesh.shape["wide"], mesh.shape["narrow"]),
        mesh=mesh,
        in_specs=(
            rows,
            flat,
            flat,
            rows,
            block,
            copied,
            copied,
            copied,
            copied,
            block,
            copied,
            block,
            copied,
            block,
            copied,
            copied,
            copied,
            block,
            copied,
            copied,
            block,
            copied,
            copied,
            copied,
            block,
            copied,
            block,
            copied,
        ),
        out_specs=(
            rows,
            rows,
            block,
            copied,
            copied,
            copied,
            copied,
            block,
            copied,
            block,
            copied,
            block,
            copied,
            copied,
            copied,
            block,
            copied,
            copied,
            block,
            copied,
            copied,
            copied,
            block,
            copied,
            block,
            copied,
        ),
        check_vma=False,
    )
```

```python
import functools

import jax
import jax.numpy as jnp
from jax import lax
from jax.experimental import pallas as pl
from jax.experimental.pallas import tpu as pltpu
from jax.sharding import PartitionSpec as P

D = 512
HEADS = 16
HD = 32
FF = 2048
CIN = 256
G = 4
NL = 256
IN_G = 512
SEGS = 4
QT = 32
PACK = 256
TILES = NL // QT
SELF_GROUPS = 2
SELF_ROWS = SELF_GROUPS * NL
CROSS_GROUPS = 4
LAT_STEP = CROSS_GROUPS * NL
IN_STEP = CROSS_GROUPS * IN_G
UNITS = 4
WIDTHS = (128, 192, 256, 384, 512)

F32 = jnp.float32
BF16 = jnp.bfloat16
NEG_FILL = -1e30
EPSILON = 1e-05
SCALE = HD**-0.5
LOG2E = 1.4426950408889634
SCALE2 = SCALE * LOG2E
VMEM_BYTES = 60 * 1024 * 1024

TAIL_RATE = 0.28
TAIL_POLY = (
    0.1165209849818009,
    0.06749547174407416,
    0.2689133347091787,
    -0.23699737809142182,
    0.38987640062523105,
    -0.10580882324798475,
)

ROW_QGAIN, ROW_QSHIFT, ROW_SOURCE, ROW_QBIAS, ROW_VBIAS = range(5)
ROW_UBIAS, ROW_COBIAS, ROW_SGAIN, ROW_SSHIFT, ROW_SQBIAS = 8, 12, 13, 14, 15
ROW_SVBIAS, ROW_SOBIAS, ROW_FGAIN, ROW_FSHIFT, ROW_DBIAS = 16, 17, 18, 19, 20
VEC_ROWS = 24
CROSS_VECS = 8
MIDDLE_VECS = VEC_ROWS - CROSS_VECS

CHUNKS = 16
HALVES = 2
CROSS_MATS = ((G * NL, D), (D, D), (CIN, 2 * D))
MIDDLE_MATS = ((D, 3 * D), (D, D), (D, FF), (FF, D), (D, D))


def slab_place(mats, at):
    sizes = [rows // CHUNKS * (columns // (HALVES * PACK)) for rows, columns in mats]
    return sum(sizes[:at]), mats[at][0] // CHUNKS, sum(sizes)


LATENT, WQ, WKV = (slab_place(CROSS_MATS, at)[:2] for at in range(3))
WPROJ, WSO, WUP, WDN, WO = (slab_place(MIDDLE_MATS, at)[:2] for at in range(5))
CROSS_SLAB = slab_place(CROSS_MATS, 0)[2]
MIDDLE_SLAB = slab_place(MIDDLE_MATS, 0)[2]


def dot_plain(left, right):
    return lax.dot_general(left, right, (((1,), (0,)), ((), ())), preferred_element_type=F32)


def dot_first(left, right):
    return lax.dot_general(left, right, (((0,), (0,)), ((), ())), preferred_element_type=F32)


def dot_last(left, right):
    return lax.dot_general(left, right, (((1,), (1,)), ((), ())), preferred_element_type=F32)


def over_rows(total, chunk, body):
    def step(index, carry):
        body(pl.ds(pl.multiple_of(index * chunk, chunk), chunk))
        return carry

    lax.fori_loop(0, total // chunk, step, 0, unroll=8)


def norm_forward(rows, gain, shift):
    centered = rows - jnp.mean(rows, -1, keepdims=True)
    rscale = lax.rsqrt(jnp.mean(centered * centered, -1, keepdims=True) + EPSILON)
    normed = centered * rscale
    return normed * gain + shift, normed, rscale


def norm_backward(grad, normed, rscale, gain):
    dnormed = grad * gain
    return rscale * (
        dnormed
        - jnp.mean(dnormed, -1, keepdims=True)
        - normed * jnp.mean(dnormed * normed, -1, keepdims=True)
    )


def column_sum(rows):
    return jnp.sum(rows, 0, keepdims=True)


def gelu_pair(hidden):
    size = jnp.abs(hidden)
    ratio = 1.0 / (1.0 + TAIL_RATE * size)
    bell = jnp.exp2(hidden * hidden * (-0.5 * LOG2E))
    poly = TAIL_POLY[-1] * ratio
    for coefficient in TAIL_POLY[-2::-1]:
        poly = (poly + coefficient) * ratio
    tail = poly * bell
    cdf = jnp.where(hidden >= 0.0, 1.0 - tail, tail)
    return hidden * cdf, cdf + hidden * bell * 0.3989422804014327


def fill_block_mask(mask_ref):
    row_head = lax.broadcasted_iota(jnp.int32, (PACK, PACK), 0) // QT
    lane_head = lax.broadcasted_iota(jnp.int32, (PACK, PACK), 1) // HD
    mask_ref[...] = jnp.where(row_head == lane_head, 1.0, 0.0).astype(BF16)


def block_diagonal(rows, mask):
    return jnp.concatenate([rows] * (PACK // QT), 0) * mask


def take_diagonal(full):
    lane = lax.broadcasted_iota(jnp.int32, (QT, 128), 1)
    columns = []
    for half in range(2):
        base = 128 * half
        picked = full[base : base + QT, base : base + 128]
        for head in range(1, 4):
            row = base + QT * head
            picked = jnp.where(
                lane >= HD * head, full[row : row + QT, base : base + 128], picked
            )
        columns.append(picked)
    return jnp.concatenate(columns, 1)


def segment_at(cuts, place):
    return sum((place >= cut).astype(jnp.int32) for cut in cuts)


def pick(index, values):
    result = values[0]
    for at in range(1, len(values)):
        result = jnp.where(index == at, values[at], result)
    return result


def in_widths(needed, body):
    smaller = 0
    for width in WIDTHS:

        @pl.when((needed > smaller) & (needed <= width))
        def _(width=width):
            body(width)

        smaller = width


def query_segments(query_cuts, tile):
    lane = lax.broadcasted_iota(jnp.int32, (1, PACK), 1) % QT
    return segment_at(query_cuts, tile * QT + lane)


def allowed_pairs(key_seg, query_seg):
    return jnp.concatenate([key_seg, key_seg], 1) == query_seg


def softmax_rows(scores, allowed):
    scores = jnp.where(allowed, scores, NEG_FILL)
    top = jnp.max(scores, 0, keepdims=True)
    powers = jnp.exp2((scores - top) * SCALE2)
    total = jnp.sum(powers, 0, keepdims=True)
    return (powers * (1.0 / total)).astype(BF16), top * SCALE2 + jnp.log2(total)


def score_grads(probs, dprobs):
    weighted = probs * dprobs
    delta = jnp.sum(weighted, 0, keepdims=True)
    return (weighted - probs * delta).astype(BF16)


def half(part):
    return slice(PACK * part, PACK * part + PACK)


def slab_part(slab_ref, place, side, piece):
    offset, rows = place
    part = slab_ref[:, side, offset + piece * rows : offset + piece * rows + rows, :]
    return part.reshape(CHUNKS * rows, PACK)


def slab_matrix(slab_ref, place, pieces):
    return jnp.concatenate(
        [
            slab_part(slab_ref, place, piece // (pieces // HALVES), piece % (pieces // HALVES))
            for piece in range(pieces)
        ],
        1,
    )


def store_halves(side, keep_ref, send_ref, place, matrix):
    offset, rows = place
    pieces = matrix.shape[1] // PACK
    inner = pieces // HALVES

    def store(refs):
        for piece in range(pieces):
            start = offset + piece % inner * rows
            part = matrix[:, piece * PACK : piece * PACK + PACK].astype(BF16)
            refs[piece // inner][:, start : start + rows, :] = part.reshape(CHUNKS, rows, PACK)

    @pl.when(side == 0)
    def _():
        store((keep_ref, send_ref))

    @pl.when(side != 0)
    def _():
        store((send_ref, keep_ref))


def latent_cuts(cuts_ref, group):
    return [cuts_ref[group, 4 + at] for at in range(SEGS - 1)]


def fill_cross_segments(seg_ref, cuts_ref, step):
    place = lax.broadcasted_iota(jnp.int32, (IN_G, 128), 0)
    for member in range(CROSS_GROUPS):
        key_cuts = [cuts_ref[step * CROSS_GROUPS + member, at] for at in range(SEGS - 1)]
        seg_ref[member * IN_G : member * IN_G + IN_G, :] = segment_at(key_cuts, place)


def cross_units(plan_ref, cuts_ref, seg_ref, step, batch, width):
    units = []
    for at in range(UNITS):
        packed = plan_ref[step, batch * UNITS + at]
        slot = packed // 1024
        start = pl.multiple_of(jnp.minimum(packed % 1024, IN_G - width), 16)
        member = slot // TILES
        tile = slot % TILES
        keys = pl.ds(pl.multiple_of(member * IN_G + start, 16), width)
        cuts = latent_cuts(cuts_ref, step * CROSS_GROUPS + member)
        allowed = allowed_pairs(seg_ref[keys, :], query_segments(cuts, tile))
        units.append((slot, pl.ds(pl.multiple_of(slot * QT, QT), QT), keys, allowed))
    return units


def batch_needed(plan_ref, step, batch):
    return plan_ref[step, CROSS_GROUPS * TILES + batch]


def plan_tiles(in_cuts, lat_cuts):
    groups = in_cuts.shape[0]
    tile = jnp.arange(TILES, dtype=jnp.int32) * QT
    first = jnp.sum(tile[None, :, None] >= lat_cuts[:, None, :], -1, dtype=jnp.int32)
    last = jnp.sum(tile[None, :, None] + (QT - 1) >= lat_cuts[:, None, :], -1, dtype=jnp.int32)
    starts = jnp.concatenate([jnp.zeros((groups, 1), jnp.int32), in_cuts], 1)
    ends = jnp.concatenate([in_cuts, jnp.full((groups, 1), IN_G, jnp.int32)], 1)
    segment = jnp.arange(SEGS, dtype=jnp.int32)
    low = jnp.sum(jnp.where(first[..., None] == segment, starts[:, None, :], 0), -1) // 16 * 16
    high = jnp.sum(jnp.where(last[..., None] == segment, ends[:, None, :], 0), -1)
    count = CROSS_GROUPS * TILES
    low = low.reshape(-1, count)
    needed = high.reshape(-1, count) - low
    slot = jnp.arange(count, dtype=jnp.int32)
    earlier = slot[:, None] < slot[None, :]
    mine, other = needed[:, None, :], needed[:, :, None]
    rank = jnp.sum((other < mine) | ((other == mine) & earlier), 1, dtype=jnp.int32)
    place = rank[:, None, :] == slot[:, None]
    packed = jnp.sum(jnp.where(place, (slot * 1024 + low)[:, None, :], 0), -1)
    batches = jnp.arange(count // UNITS, dtype=jnp.int32)[:, None]
    inside = rank[:, None, :] // UNITS == batches
    widest = jnp.max(jnp.where(inside, needed[:, None, :], 0), -1)
    return jnp.concatenate([packed, widest], 1).astype(jnp.int32)


def cross_forward_kernel(
    cuts_ref,
    plan_ref,
    source_ref,
    slab_ref,
    vec_ref,
    mix_ref,
    kv_ref,
    lse_ref,
    query_ref,
    latent_ref,
    mask_ref,
    seg_ref,
):
    step = pl.program_id(0)

    @pl.when(step == 0)
    def _():
        fill_block_mask(mask_ref)
        latent = slab_matrix(slab_ref, LATENT, 2)
        latent_ref[...] = latent
        low, _, _ = norm_forward(
            latent.astype(F32),
            vec_ref[ROW_QGAIN : ROW_QGAIN + 1, :],
            vec_ref[ROW_QSHIFT : ROW_QSHIFT + 1, :],
        )
        query = dot_plain(low.astype(BF16), slab_matrix(slab_ref, WQ, 2))
        query_ref[...] = (query + vec_ref[ROW_QBIAS : ROW_QBIAS + 1, :]).astype(BF16)

    wkv = slab_matrix(slab_ref, WKV, 4)
    kv_ref[:, :D] = dot_plain(source_ref[...], wkv[:, :D]).astype(BF16)
    kv_ref[:, D:] = (
        dot_plain(source_ref[...], wkv[:, D:]) + vec_ref[ROW_VBIAS : ROW_VBIAS + 1, :]
    ).astype(BF16)

    fill_cross_segments(seg_ref, cuts_ref, step)

    def batch_body(batch, carry):
        def window(width):
            units = cross_units(plan_ref, cuts_ref, seg_ref, step, batch, width)
            scores = [
                dot_last(
                    kv_ref[keys, half(part)],
                    block_diagonal(query_ref[rows, half(part)], mask_ref[...]),
                )
                for _, rows, keys, _ in units
                for part in range(2)
            ]
            probs = []
            for at, (slot, _, _, allowed) in enumerate(units):
                for part in range(2):
                    low, lse = softmax_rows(scores[2 * at + part], allowed)
                    probs.append(low)
                    lse_ref[pl.ds(slot * 2 + part, 1), :] = lse
            for at, (_, rows, keys, _) in enumerate(units):
                for part in range(2):
                    full = dot_first(probs[2 * at + part], kv_ref[keys, half(part + 2)])
                    mix_ref[rows, half(part)] = take_diagonal(full).astype(BF16)

        in_widths(batch_needed(plan_ref, step, batch), window)
        return carry

    lax.fori_loop(0, CROSS_GROUPS * TILES // UNITS, batch_body, 0)


def middle_kernel(
    cuts_ref,
    side_ref,
    cross_mix_ref,
    cot_ref,
    latent_ref,
    slab_ref,
    vec_ref,
    active_ref,
    after_self_ref,
    dcross_mix_ref,
    glat_ref,
    small_ref,
    keep_ref,
    send_ref,
    mask_ref,
    after_ref,
    hat1_ref,
    rs1_ref,
    low1_ref,
    triple_ref,
    probs_ref,
    mix_ref,
    res_ref,
    hat2_ref,
    rs2_ref,
    low2_ref,
    dtop_ref,
    dso_ref,
    dmix_ref,
    dtriple_ref,
    aproj_ref,
    aso_ref,
    aup_ref,
    adn_ref,
    ao_ref,
):
    step = pl.program_id(0)
    last = pl.num_programs(0) - 1

    def vec(row):
        return vec_ref[row : row + 1, :]

    def add_small(row, value):
        small_ref[row - CROSS_VECS : row - CROSS_VECS + 1, :] += value

    @pl.when(step == 0)
    def _():
        fill_block_mask(mask_ref)
        for ref in (glat_ref, small_ref, aproj_ref, aso_ref, aup_ref, adn_ref, ao_ref):
            ref[...] = jnp.zeros(ref.shape, ref.dtype)

    base = pl.multiple_of(step % (G // SELF_GROUPS) * SELF_ROWS, SELF_ROWS)
    after_ref[...] = (
        latent_ref[pl.ds(base, SELF_ROWS), :].astype(F32)
        + dot_plain(cross_mix_ref[...], slab_matrix(slab_ref, WO, 2))
        + vec(ROW_COBIAS)
    )

    def first_norm(rows):
        low, normed, rscale = norm_forward(after_ref[rows, :], vec(ROW_SGAIN), vec(ROW_SSHIFT))
        low1_ref[rows, :] = low.astype(BF16)
        hat1_ref[rows, :] = normed
        rs1_ref[rows, :] = rscale

    over_rows(SELF_ROWS, 64, first_norm)
    wproj = slab_matrix(slab_ref, WPROJ, 6)
    for block, bias in enumerate((ROW_SQBIAS, None, ROW_SVBIAS)):
        columns = slice(D * block, D * block + D)
        product = dot_plain(low1_ref[...], wproj[:, columns])
        if bias is not None:
            product = product + vec(bias)
        triple_ref[:, columns] = product.astype(BF16)

    units = [(member, part) for member in range(SELF_GROUPS) for part in range(2)]

    def group_rows(member):
        return slice(member * NL, member * NL + NL)

    def block_rows(ref, member, part):
        starts = range(member * NL, member * NL + NL, QT)
        return jnp.concatenate(
            [block_diagonal(ref[at : at + QT, half(part)], mask_ref[...]) for at in starts], 0
        )

    def unit_scores(member, part):
        keys = triple_ref[group_rows(member), half(part + 2)]
        return dot_last(block_rows(triple_ref, member, part), keys)

    ahead = unit_scores(*units[0])
    for at, (member, part) in enumerate(units):
        scores = ahead
        if at + 1 < len(units):
            ahead = unit_scores(*units[at + 1])
        cuts = latent_cuts(cuts_ref, step * SELF_GROUPS + member)
        key_seg = segment_at(cuts, lax.broadcasted_iota(jnp.int32, (QT, NL), 1))
        place = lax.broadcasted_iota(jnp.int32, (QT, NL), 0)
        probs = []
        for tile in range(TILES):
            allowed = segment_at(cuts, tile * QT + place) == key_seg
            block = scores[tile * PACK : tile * PACK + PACK].reshape(PACK // QT, QT, NL)
            block = jnp.where(allowed[None], block, NEG_FILL)
            top = jnp.max(block, 2, keepdims=True)
            powers = jnp.exp2((block - top) * SCALE2)
            total = jnp.sum(powers, 2, keepdims=True)
            probs.append((powers * (1.0 / total)).reshape(PACK, NL).astype(BF16))
        probs = jnp.concatenate(probs, 0)
        probs_ref[member * 2 + part] = probs
        full = dot_plain(probs, triple_ref[group_rows(member), half(part + 4)])
        for tile in range(TILES):
            rows = slice(member * NL + tile * QT, member * NL + tile * QT + QT)
            mixed = take_diagonal(full[tile * PACK : tile * PACK + PACK])
            mix_ref[rows, half(part)] = mixed.astype(BF16)

    after_self_ref[...] = after_ref[...] + dot_plain(mix_ref[...], slab_matrix(slab_ref, WSO, 2)) + vec(ROW_SOBIAS)

    def second_norm(rows):
        low, normed, rscale = norm_forward(after_self_ref[rows, :], vec(ROW_FGAIN), vec(ROW_FSHIFT))
        low2_ref[rows, :] = low.astype(BF16)
        hat2_ref[rows, :] = normed
        rs2_ref[rows, :] = rscale

    over_rows(SELF_ROWS, 64, second_norm)
    dtop_ref[...] = jnp.zeros(dtop_ref.shape, F32)

    def feed_front(block):
        up = slab_part(slab_ref, WUP, *divmod(block, FF // PACK // HALVES))
        offset, height = WDN
        chunks = slice(block * PACK // height, (block + 1) * PACK // height)
        down = jnp.concatenate(
            [
                slab_ref[chunks, side, offset : offset + height, :].reshape(PACK, PACK)
                for side in range(HALVES)
            ],
            1,
        )
        row, column = divmod(block * PACK, D)
        bias = vec_ref[ROW_UBIAS + row : ROW_UBIAS + row + 1, column : column + PACK]
        hidden = dot_plain(low2_ref[...], up) + bias
        return up, down, hidden, dot_last(cot_ref[...], down)

    ahead = feed_front(0)
    for block in range(FF // PACK):
        up, down, hidden, dactive = ahead
        if block + 1 < FF // PACK:
            ahead = feed_front(block + 1)
        active, slope = gelu_pair(hidden)
        active = active.astype(BF16)
        dhidden = slope * dactive
        row, column = divmod(block * PACK, D)
        row += ROW_UBIAS - CROSS_VECS
        small_ref[row : row + 1, column : column + PACK] += column_sum(dhidden)
        dhidden = dhidden.astype(BF16)
        columns = slice(block * PACK, block * PACK + PACK)
        adn_ref[columns, :] += dot_first(active, cot_ref[...])
        aup_ref[:, columns] += dot_first(low2_ref[...], dhidden)
        active_ref[:, columns] = active
        dtop_ref[...] += dot_last(dhidden, up)

    def after_feed(rows):
        dtop = dtop_ref[rows, :]
        normed = hat2_ref[rows, :]
        cot = cot_ref[rows, :].astype(F32)
        dafter = cot + norm_backward(dtop, normed, rs2_ref[rows, :], vec(ROW_FGAIN))
        dlow = dafter.astype(BF16)
        res_ref[rows, :] = dafter
        dso_ref[rows, :] = dlow
        add_small(ROW_FGAIN, column_sum(dtop * normed))
        add_small(ROW_FSHIFT, column_sum(dtop))
        add_small(ROW_DBIAS, column_sum(cot))
        add_small(ROW_SOBIAS, column_sum(dlow.astype(F32)))

    over_rows(SELF_ROWS, 64, after_feed)
    aso_ref[...] += dot_first(mix_ref[...], dso_ref[...])
    dmix_ref[...] = dot_last(dso_ref[...], slab_matrix(slab_ref, WSO, 2)).astype(BF16)

    def unit_dprobs(member, part):
        grads = block_rows(dmix_ref, member, part)
        values = triple_ref[group_rows(member), half(part + 4)]
        return grads, dot_last(grads, values)

    ahead = unit_dprobs(*units[0])
    for at, (member, part) in enumerate(units):
        grads, dprobs = ahead
        if at + 1 < len(units):
            ahead = unit_dprobs(*units[at + 1])
        group = group_rows(member)
        probs = probs_ref[member * 2 + part]
        dtriple_ref[group, half(part + 4)] = dot_first(probs, grads).astype(BF16)
        dscores = []
        for tile in range(TILES):
            rows = slice(tile * PACK, tile * PACK + PACK)
            block = probs[rows].astype(F32)
            weighted = block * dprobs[rows]
            delta = jnp.sum(weighted, 1, keepdims=True)
            dscores.append((weighted - block * delta).astype(BF16))
        dscores = jnp.concatenate(dscores, 0)
        dkeys = dot_first(dscores, block_rows(triple_ref, member, part))
        dtriple_ref[group, half(part + 2)] = (dkeys * SCALE).astype(BF16)
        full = dot_plain(dscores, triple_ref[group, half(part + 2)])
        for tile in range(TILES):
            rows = slice(member * NL + tile * QT, member * NL + tile * QT + QT)
            dquery = take_diagonal(full[tile * PACK : tile * PACK + PACK])
            dtriple_ref[rows, half(part)] = (dquery * SCALE).astype(BF16)
    for block in range(3):
        columns = slice(D * block, D * block + D)
        aproj_ref[:, columns] += dot_first(low1_ref[...], dtriple_ref[:, columns])
    add_small(ROW_SQBIAS, column_sum(dtriple_ref[:, :D].astype(F32)))
    add_small(ROW_SVBIAS, column_sum(dtriple_ref[:, 2 * D :].astype(F32)))
    dtop_ref[...] = dot_last(dtriple_ref[...], slab_matrix(slab_ref, WPROJ, 6))

    def after_self(rows):
        dmid = dtop_ref[rows, :]
        normed = hat1_ref[rows, :]
        dafter = res_ref[rows, :] + norm_backward(dmid, normed, rs1_ref[rows, :], vec(ROW_SGAIN))
        dlow = dafter.astype(BF16)
        dso_ref[rows, :] = dlow
        glat_ref[pl.ds(pl.multiple_of(base + rows.start, 64), rows.size), :] += dafter
        add_small(ROW_SGAIN, column_sum(dmid * normed))
        add_small(ROW_SSHIFT, column_sum(dmid))
        add_small(ROW_COBIAS, column_sum(dlow.astype(F32)))

    over_rows(SELF_ROWS, 64, after_self)
    ao_ref[...] += dot_first(cross_mix_ref[...], dso_ref[...])
    dcross_mix_ref[...] = dot_last(dso_ref[...], slab_matrix(slab_ref, WO, 2)).astype(BF16)

    @pl.when(step == last)
    def _():
        side = side_ref[0]
        store_halves(side, keep_ref, send_ref, WPROJ, aproj_ref[...])
        store_halves(side, keep_ref, send_ref, WSO, aso_ref[...])
        store_halves(side, keep_ref, send_ref, WUP, aup_ref[...])
        store_halves(side, keep_ref, send_ref, WDN, adn_ref[...])
        store_halves(side, keep_ref, send_ref, WO, ao_ref[...])


def row_dot(rows, matrix):
    high = rows.astype(BF16)
    low = (rows - high.astype(F32)).astype(BF16)
    return dot_last(high, matrix) + dot_last(low, matrix)


def row_sums(matrix):
    high = matrix.astype(BF16)
    low = (matrix - high.astype(F32)).astype(BF16)
    ones = jnp.ones((8, matrix.shape[1]), BF16)
    return (dot_last(ones, high) + dot_last(ones, low))[:1]


VECTOR_PLACES = (
    (ROW_QGAIN, 0),
    (ROW_QSHIFT, 0),
    (ROW_SOURCE, 0),
    (ROW_SOURCE, CIN),
    (ROW_QBIAS, 0),
    (ROW_VBIAS, 0),
    (ROW_COBIAS, 0),
    (ROW_SGAIN, 0),
    (ROW_SSHIFT, 0),
    (ROW_SQBIAS, 0),
    (ROW_SVBIAS, 0),
    (ROW_SOBIAS, 0),
    (ROW_FGAIN, 0),
    (ROW_FSHIFT, 0),
    (ROW_UBIAS, 0),
    (ROW_DBIAS, 0),
)


def cross_backward_kernel(
    cuts_ref,
    plan_ref,
    side_ref,
    source_ref,
    kv_ref,
    lse_ref,
    dmix_ref,
    query_ref,
    glat_ref,
    slab_ref,
    vec_ref,
    dkv_ref,
    keep_ref,
    send_ref,
    small_ref,
    mask_ref,
    seg_ref,
    dkey_ref,
    dvalue_ref,
    dquery_ref,
    akv_ref,
    dsum_ref,
):
    step = pl.program_id(0)
    last = pl.num_programs(0) - 1

    def vec(row):
        return vec_ref[row : row + 1, :]

    def add_small(row, value):
        small_ref[row : row + 1, :] += value

    def add_row(ref, value):
        ref[...] += value

    @pl.when(step == 0)
    def _():
        fill_block_mask(mask_ref)
        for ref in (small_ref, dquery_ref, akv_ref, dsum_ref):
            ref[...] = jnp.zeros(ref.shape, ref.dtype)

    fill_cross_segments(seg_ref, cuts_ref, step)
    dkey_ref[...] = jnp.zeros(dkey_ref.shape, F32)
    dvalue_ref[...] = jnp.zeros(dvalue_ref.shape, F32)

    def batch_body(batch, carry):
        def window(width):
            units = cross_units(plan_ref, cuts_ref, seg_ref, step, batch, width)
            work = []
            for slot, rows, keys, allowed in units:
                for part in range(2):
                    queries = block_diagonal(query_ref[rows, half(part)], mask_ref[...])
                    grads = block_diagonal(dmix_ref[rows, half(part)], mask_ref[...])
                    scores = dot_last(kv_ref[keys, half(part)], queries)
                    dprobs = dot_last(kv_ref[keys, half(part + 2)], grads)
                    work.append((slot, rows, keys, allowed, part, queries, grads, scores, dprobs))
            ready = []
            for slot, rows, keys, allowed, part, queries, grads, scores, dprobs in work:
                lse = lse_ref[pl.ds(slot * 2 + part, 1), :]
                probs = jnp.exp2(jnp.where(allowed, scores * SCALE2 - lse, NEG_FILL))
                dscores = score_grads(probs, dprobs)
                ready.append((rows, keys, part, queries, grads, probs.astype(BF16), dscores))
            for rows, keys, part, queries, grads, probs, dscores in ready:
                dvalue_ref[keys, half(part)] += dot_plain(probs, grads)
                dkey_ref[keys, half(part)] += dot_plain(dscores, queries)
                dquery_ref[rows, half(part)] += take_diagonal(
                    dot_first(dscores, kv_ref[keys, half(part)])
                )

        in_widths(batch_needed(plan_ref, step, batch), window)
        return carry

    lax.fori_loop(0, CROSS_GROUPS * TILES // UNITS, batch_body, 0)
    dkv_ref[:, :D] = (dkey_ref[...] * SCALE).astype(BF16)
    dkv_ref[:, D:] = dvalue_ref[...].astype(BF16)

    for part in range(2):
        columns = slice(D * part, D * part + D)
        akv_ref[:, columns] += dot_first(source_ref[...], dkv_ref[:, columns])
    over_rows(IN_STEP, 256, lambda rows: add_row(dsum_ref, column_sum(dkv_ref[rows, :].astype(F32))))

    @pl.when(step == last)
    def _():
        side = side_ref[0]
        store_halves(side, keep_ref, send_ref, WKV, akv_ref[...])
        wkv = slab_matrix(slab_ref, WKV, 4)
        sums = dsum_ref[...]
        add_small(ROW_VBIAS, sums[:, D:])
        shift_grad = row_dot(jnp.broadcast_to(sums, (8, 2 * D)), wkv)[:1]
        product = wkv.astype(F32) * akv_ref[...]
        both = row_sums(product)
        gain = vec_ref[ROW_SOURCE : ROW_SOURCE + 1, :CIN]
        shift = vec_ref[ROW_SOURCE : ROW_SOURCE + 1, CIN:]
        small_ref[ROW_SOURCE : ROW_SOURCE + 1, :CIN] = (both - shift * shift_grad) / gain
        small_ref[ROW_SOURCE : ROW_SOURCE + 1, CIN:] = shift_grad
        low, normed, rscale = norm_forward(
            slab_matrix(slab_ref, LATENT, 2).astype(F32), vec(ROW_QGAIN), vec(ROW_QSHIFT)
        )
        dquery = (dquery_ref[...] * SCALE).astype(BF16)
        store_halves(side, keep_ref, send_ref, WQ, dot_first(low.astype(BF16), dquery))
        add_small(ROW_QBIAS, column_sum(dquery.astype(F32)))
        dnorm = dot_last(dquery, slab_matrix(slab_ref, WQ, 2))
        add_small(ROW_QGAIN, column_sum(dnorm * normed))
        add_small(ROW_QSHIFT, column_sum(dnorm))
        total = glat_ref[...] + norm_backward(dnorm, normed, rscale, vec(ROW_QGAIN))
        store_halves(side, keep_ref, send_ref, LATENT, total)


def output_kernel(active_ref, after_self_ref, slab_ref, vec_ref, out_ref):
    total = after_self_ref[...] + dot_plain(active_ref[...], slab_matrix(slab_ref, WDN, 2))
    out_ref[...] = (total + vec_ref[ROW_DBIAS : ROW_DBIAS + 1, :]).astype(BF16)


def source_kernel(inputs_ref, dkv_ref, slab_ref, vec_ref, dinput_ref):
    gain = vec_ref[ROW_SOURCE : ROW_SOURCE + 1, :CIN]
    shift = vec_ref[ROW_SOURCE : ROW_SOURCE + 1, CIN:]
    wkv = slab_matrix(slab_ref, WKV, 4)

    def source_back(rows):
        dsource = dot_last(dkv_ref[rows, :], wkv)
        _, normed, rscale = norm_forward(inputs_ref[rows, :].astype(F32), gain, shift)
        dinput_ref[rows, :] = norm_backward(dsource, normed, rscale, gain)

    over_rows(IN_STEP, 256, source_back)


def pack_kernel(*refs):
    cross, middle = refs[: len(CROSS_MATS)], refs[len(CROSS_MATS) : -2]
    copies_ref, packed_ref = refs[-2:]
    for targets, shards in (((copies_ref, True), cross), ((packed_ref, False), middle)):
        target_ref, copied = targets
        start = 0
        for shard in shards:
            rows, columns = shard.shape
            for column in range(0, columns, PACK):
                part = shard[:, column : column + PACK]
                if copied:
                    part = jnp.broadcast_to(part, (CHUNKS, rows, PACK))
                    target_ref[:, start : start + rows, :] = part
                else:
                    target_ref[start : start + rows, :] = part
                start += rows


def combine_kernel(keep_ref, sent_ref, small_ref, small_sent_ref, out_ref):
    total = keep_ref[...].astype(F32) + sent_ref[...].astype(F32)
    out_ref[:, :CROSS_SLAB, :] = total.astype(BF16)
    small = small_ref[...] + small_sent_ref[...]
    small = jnp.concatenate([small[:, :PACK], small[:, PACK:]], 0)
    high = small.astype(BF16)
    low = (small - high.astype(F32)).astype(BF16)
    rows = 2 * CROSS_VECS
    for at, part in enumerate((high, low)):
        start = CROSS_SLAB + at * rows
        out_ref[:, start : start + rows, :] = jnp.broadcast_to(part, (CHUNKS, rows, PACK))


def finish_kernel(parts_ref, middle_ref, small_ref, *outs):
    mats, vectors = outs[: len(CROSS_MATS) + len(MIDDLE_MATS)], outs[-16:]
    total = parts_ref[0].astype(F32)
    for at in range(1, CHUNKS):
        total = total + parts_ref[at].astype(F32)
    middle = middle_ref[...].astype(F32)
    for source, shards in ((total, mats[: len(CROSS_MATS)]), (middle, mats[len(CROSS_MATS) :])):
        start = 0
        for shard in shards:
            rows, columns = shard.shape
            for column in range(0, columns, PACK):
                shard[:, column : column + PACK] = source[start : start + rows]
                start += rows
    rows = 2 * CROSS_VECS
    small = total[CROSS_SLAB : CROSS_SLAB + rows] + total[CROSS_SLAB + rows :]
    small = jnp.concatenate([small[:CROSS_VECS], small[CROSS_VECS:]], 1)
    write_vectors(jnp.concatenate([small, jnp.sum(small_ref[...], 0)], 0), vectors)


def write_vectors(rows, vectors):
    for ref, (row, start) in zip(vectors, VECTOR_PLACES):
        size = ref.shape[-1]
        taken = [
            rows[row + at : row + at + 1, start : start + min(size, D)]
            for at in range(max(1, size // D))
        ]
        ref[...] = jnp.concatenate(taken, 1)


def rows_spec(rows, columns):
    return pl.BlockSpec((rows, columns), lambda step, *scalars: (step, 0))


def whole_spec(rows, columns):
    return pl.BlockSpec(
        (rows, columns), lambda step, *scalars: (0, 0), pipeline_mode=pl.Buffered(1)
    )


def kernel_call(kernel, scalars, steps, in_specs, out_specs, out_shape, scratch, flops):
    return pl.pallas_call(
        kernel,
        grid_spec=pltpu.PrefetchScalarGridSpec(
            num_scalar_prefetch=scalars,
            grid=(steps,),
            in_specs=in_specs,
            out_specs=out_specs,
            scratch_shapes=scratch,
        ),
        out_shape=out_shape,
        compiler_params=pltpu.CompilerParams(
            vmem_limit_bytes=VMEM_BYTES, dimension_semantics=("arbitrary",)
        ),
        cost_estimate=pl.CostEstimate(
            flops=flops, bytes_accessed=100 * 2**20, transcendentals=0
        ),
    )


def slab_spec(rows):
    return pl.BlockSpec(
        (CHUNKS, HALVES, rows, PACK),
        lambda step, *scalars: (0, 0, 0, 0),
        pipeline_mode=pl.Buffered(1),
    )


def slab_shape(rows):
    return jax.ShapeDtypeStruct((CHUNKS, HALVES, rows, PACK), BF16)


def gather_whole(shards):
    parts = []
    for shard in shards:
        full = lax.all_gather(
            lax.all_gather(shard, "narrow", axis=1, tiled=True), "wide", axis=0, tiled=True
        )
        rows, columns = full.shape
        split = full.reshape(CHUNKS, rows // CHUNKS, HALVES, columns // (HALVES * PACK), PACK)
        parts.append(split.transpose(0, 2, 3, 1, 4).reshape(CHUNKS, HALVES, -1, PACK))
    return jnp.concatenate(parts, 2)


def scatter_whole(slab, mats):
    shards = []
    start = 0
    for rows, columns in mats:
        height = rows // CHUNKS
        pieces = columns // (HALVES * PACK)
        part = slab[:, :, start : start + height * pieces]
        start += height * pieces
        part = part.reshape(CHUNKS, HALVES, pieces, height, PACK).transpose(0, 3, 1, 2, 4)
        total = lax.psum_scatter(
            part.reshape(rows, columns), "wide", scatter_dimension=0, tiled=True
        )
        total = lax.psum_scatter(total, "narrow", scatter_dimension=1, tiled=True)
        shards.append(total.astype(F32))
    return shards


SWAP = ((0, 1), (1, 0))


def simple_call(kernel, out_shape):
    return pl.pallas_call(
        kernel,
        out_shape=out_shape,
        compiler_params=pltpu.CompilerParams(vmem_limit_bytes=VMEM_BYTES),
    )


def half_shape(rows):
    return jax.ShapeDtypeStruct((CHUNKS, rows, PACK), BF16)


def half_spec(rows):
    return pl.BlockSpec(
        (CHUNKS, rows, PACK), lambda step, *scalars: (0, 0, 0), pipeline_mode=pl.Buffered(1)
    )


def gather_soon(copies):
    mine = lax.all_to_all(copies, "wide", 0, 0)
    other = lax.ppermute(mine, "narrow", SWAP)
    first = lax.axis_index("narrow") == 0
    return jnp.stack([jnp.where(first, mine, other), jnp.where(first, other, mine)], 1)


def gather_later(packed):
    full = lax.all_gather(packed, ("wide", "narrow"), axis=0)
    return full.reshape((CHUNKS, HALVES) + packed.shape)


def scatter_later(keep, send):
    sent = lax.ppermute(send, "narrow", SWAP)
    total = (keep.astype(F32) + sent.astype(F32)).astype(BF16)
    return lax.psum_scatter(total, "wide", scatter_dimension=0)


def scatter_soon(keep, send, small):
    sent = lax.ppermute(send, "narrow", SWAP)
    small_sent = lax.ppermute(small, "narrow", SWAP)
    rows = CROSS_SLAB + 4 * CROSS_VECS
    combined = simple_call(combine_kernel, half_shape(rows))(keep, sent, small, small_sent)
    return lax.all_to_all(combined, "wide", 0, 0)


def shape(rows, columns, dtype):
    return jax.ShapeDtypeStruct((rows, columns), dtype)


def local(
    wide,
    narrow,
    inputs,
    input_segments,
    latent_segments,
    cotangent,
    latent_array,
    query_gain,
    query_shift,
    source_gain,
    source_shift,
    cross_query,
    cross_qbias,
    cross_keyval,
    cross_vbias,
    cross_output,
    cross_obias,
    self_gain,
    self_shift,
    self_project,
    self_qbias,
    self_vbias,
    self_output,
    self_obias,
    feed_gain,
    feed_shift,
    feed_upward,
    feed_ubias,
    feed_downward,
    feed_dbias,
):
    lat_rows = cotangent.shape[0]
    in_rows = inputs.shape[0]
    groups = lat_rows // NL
    steps = groups // CROSS_GROUPS
    self_steps = groups // SELF_GROUPS

    vectors = jnp.concatenate(
        [
            query_gain,
            query_shift,
            source_gain,
            source_shift,
            cross_qbias,
            cross_vbias,
            jnp.zeros(((ROW_UBIAS - ROW_VBIAS - 1) * D,), BF16),
            feed_ubias,
            cross_obias,
            self_gain,
            self_shift,
            self_qbias,
            self_vbias,
            self_obias,
            feed_gain,
            feed_shift,
            feed_dbias,
            jnp.zeros(((VEC_ROWS - ROW_DBIAS - 1) * D,), BF16),
        ]
    )
    vectors = vectors.astype(F32).reshape(VEC_ROWS, D)
    marks = jnp.arange(1, SEGS, dtype=jnp.int32)
    in_cuts = jnp.sum(input_segments.reshape(groups, IN_G, 1) < marks, 1, dtype=jnp.int32)
    lat_cuts = jnp.sum(latent_segments.reshape(groups, NL, 1) < marks, 1, dtype=jnp.int32)
    blank = jnp.zeros((groups, 1), jnp.int32)
    cuts = jnp.concatenate([in_cuts, blank, lat_cuts, blank], 1)
    plan = plan_tiles(in_cuts, lat_cuts)

    source_low, _, _ = norm_forward(
        inputs.astype(F32), source_gain.astype(F32), source_shift.astype(F32)
    )
    source_low = source_low.astype(BF16)

    cross_shards = (latent_array, cross_query, cross_keyval)
    middle_shards = (self_project, self_output, feed_upward, feed_downward, cross_output)
    packed = (wide, narrow) == (CHUNKS, HALVES)
    if packed:
        copies, middle_packed = simple_call(
            pack_kernel, [half_shape(CROSS_SLAB), shape(MIDDLE_SLAB, PACK, BF16)]
        )(*cross_shards, *middle_shards)
        cross_slab = gather_soon(copies)
        middle_slab = gather_later(middle_packed)
        side = lax.axis_index("narrow").astype(jnp.int32).reshape(1)
    else:
        cross_slab = gather_whole(cross_shards)
        middle_slab = gather_whole(middle_shards)
        side = jnp.zeros((1,), jnp.int32)

    vec_spec = whole_spec(VEC_ROWS, D)
    lse_rows = CROSS_GROUPS * TILES * 2
    cross_mix, keyval, lse, query, latent_full = kernel_call(
        cross_forward_kernel,
        2,
        steps,
        [rows_spec(IN_STEP, CIN), slab_spec(CROSS_SLAB), vec_spec],
        [
            rows_spec(LAT_STEP, D),
            rows_spec(IN_STEP, 2 * D),
            rows_spec(lse_rows, PACK),
            whole_spec(G * NL, D),
            whole_spec(G * NL, D),
        ],
        [
            shape(lat_rows, D, BF16),
            shape(in_rows, 2 * D, BF16),
            shape(steps * lse_rows, PACK, F32),
            shape(G * NL, D, BF16),
            shape(G * NL, D, BF16),
        ],
        [
            pltpu.VMEM((PACK, PACK), BF16),
            pltpu.VMEM((IN_STEP, 128), jnp.int32),
        ],
        60 * 10**9,
    )(cuts, plan, source_low, cross_slab, vectors)

    active, after_self, dcross_mix, glat, middle_small, middle_keep, middle_send = kernel_call(
        middle_kernel,
        2,
        self_steps,
        [
            rows_spec(SELF_ROWS, D),
            rows_spec(SELF_ROWS, D),
            whole_spec(G * NL, D),
            slab_spec(MIDDLE_SLAB),
            vec_spec,
        ],
        [
            rows_spec(SELF_ROWS, FF),
            rows_spec(SELF_ROWS, D),
            rows_spec(SELF_ROWS, D),
            whole_spec(G * NL, D),
            whole_spec(MIDDLE_VECS, D),
            half_spec(MIDDLE_SLAB),
            half_spec(MIDDLE_SLAB),
        ],
        [
            shape(lat_rows, FF, BF16),
            shape(lat_rows, D, F32),
            shape(lat_rows, D, BF16),
            shape(G * NL, D, F32),
            shape(MIDDLE_VECS, D, F32),
            half_shape(MIDDLE_SLAB),
            half_shape(MIDDLE_SLAB),
        ],
        [
            pltpu.VMEM((PACK, PACK), BF16),
            pltpu.VMEM((SELF_ROWS, D), F32),
            pltpu.VMEM((SELF_ROWS, D), F32),
            pltpu.VMEM((SELF_ROWS, 1), F32),
            pltpu.VMEM((SELF_ROWS, D), BF16),
            pltpu.VMEM((SELF_ROWS, 3 * D), BF16),
            pltpu.VMEM((SELF_GROUPS * 2, TILES * PACK, NL), BF16),
            pltpu.VMEM((SELF_ROWS, D), BF16),
            pltpu.VMEM((SELF_ROWS, D), F32),
            pltpu.VMEM((SELF_ROWS, D), F32),
            pltpu.VMEM((SELF_ROWS, 1), F32),
            pltpu.VMEM((SELF_ROWS, D), BF16),
            pltpu.VMEM((SELF_ROWS, D), F32),
            pltpu.VMEM((SELF_ROWS, D), BF16),
            pltpu.VMEM((SELF_ROWS, D), BF16),
            pltpu.VMEM((SELF_ROWS, 3 * D), BF16),
            pltpu.VMEM((D, 3 * D), F32),
            pltpu.VMEM((D, D), F32),
            pltpu.VMEM((D, FF), F32),
            pltpu.VMEM((FF, D), F32),
            pltpu.VMEM((D, D), F32),
        ],
        250 * 10**9,
    )(cuts, side, cross_mix, cotangent, latent_full, middle_slab, vectors)

    dkeyval, cross_keep, cross_send, cross_small = kernel_call(
        cross_backward_kernel,
        3,
        steps,
        [
            rows_spec(IN_STEP, CIN),
            rows_spec(IN_STEP, 2 * D),
            rows_spec(lse_rows, PACK),
            rows_spec(LAT_STEP, D),
            whole_spec(G * NL, D),
            whole_spec(G * NL, D),
            slab_spec(CROSS_SLAB),
            vec_spec,
        ],
        [
            rows_spec(IN_STEP, 2 * D),
            half_spec(CROSS_SLAB),
            half_spec(CROSS_SLAB),
            whole_spec(CROSS_VECS, D),
        ],
        [
            shape(in_rows, 2 * D, BF16),
            half_shape(CROSS_SLAB),
            half_shape(CROSS_SLAB),
            shape(CROSS_VECS, D, F32),
        ],
        [
            pltpu.VMEM((PACK, PACK), BF16),
            pltpu.VMEM((IN_STEP, 128), jnp.int32),
            pltpu.VMEM((IN_STEP, D), F32),
            pltpu.VMEM((IN_STEP, D), F32),
            pltpu.VMEM((G * NL, D), F32),
            pltpu.VMEM((CIN, 2 * D), F32),
            pltpu.VMEM((1, 2 * D), F32),
        ],
        100 * 10**9,
    )(cuts, plan, side, source_low, keyval, lse, dcross_mix, query, glat, cross_slab, vectors)

    late_vectors, _ = lax.optimization_barrier((vectors, cross_small))
    latents_out = kernel_call(
        output_kernel,
        0,
        self_steps,
        [
            rows_spec(SELF_ROWS, FF),
            rows_spec(SELF_ROWS, D),
            slab_spec(MIDDLE_SLAB),
            vec_spec,
        ],
        rows_spec(SELF_ROWS, D),
        shape(lat_rows, D, BF16),
        [],
        13 * 10**9,
    )(active, after_self, middle_slab, late_vectors)

    dinput = kernel_call(
        source_kernel,
        0,
        steps,
        [rows_spec(IN_STEP, CIN), rows_spec(IN_STEP, 2 * D), slab_spec(CROSS_SLAB), vec_spec],
        rows_spec(IN_STEP, CIN),
        shape(in_rows, CIN, F32),
        [],
        20 * 10**9,
    )(inputs, dkeyval, cross_slab, vectors)

    axes = ("wide", "narrow")
    vector_sizes = [D, D, CIN, CIN] + [D] * 10 + [FF, D]
    if packed:
        middle_total = scatter_later(middle_keep, middle_send)
        small_all = lax.all_gather(middle_small, axes, axis=0)
        parts = scatter_soon(cross_keep, cross_send, cross_small)
        mats = [
            shape(rows // CHUNKS, columns // HALVES, F32)
            for rows, columns in CROSS_MATS + MIDDLE_MATS
        ]
        results = simple_call(
            finish_kernel, mats + [shape(1, size, F32) for size in vector_sizes]
        )(parts, middle_total, small_all)
        glatent, gq, gkv, gproj, gso, gup, gdn, go = results[:8]
        sums = [row.reshape(-1) for row in results[8:]]
    else:
        cross_grads = jnp.stack([cross_keep, cross_send], 1)
        middle_grads = jnp.stack([middle_keep, middle_send], 1)
        glatent, gq, gkv = scatter_whole(cross_grads, CROSS_MATS)
        gproj, gso, gup, gdn, go = scatter_whole(middle_grads, MIDDLE_MATS)
        total = lax.psum(jnp.concatenate([cross_small, middle_small], 0), axes).reshape(-1)
        sums = [
            total[row * D + start : row * D + start + size]
            for (row, start), size in zip(VECTOR_PLACES, vector_sizes)
        ]

    return (
        latents_out,
        dinput,
        glatent,
        *sums[:4],
        gq,
        sums[4],
        gkv,
        sums[5],
        go,
        *sums[6:9],
        gproj,
        *sums[9:11],
        gso,
        *sums[11:14],
        gup,
        sums[14],
        gdn,
        sums[15],
    )


def solution(mesh):
    rows = P(("wide", "narrow"), None)
    flat = P(("wide", "narrow"))
    block = P("wide", "narrow")
    copied = P()
    return jax.shard_map(
        functools.partial(local, mesh.shape["wide"], mesh.shape["narrow"]),
        mesh=mesh,
        in_specs=(
            rows,
            flat,
            flat,
            rows,
            block,
            copied,
            copied,
            copied,
            copied,
            block,
            copied,
            block,
            copied,
            block,
            copied,
            copied,
            copied,
            block,
            copied,
            copied,
            block,
            copied,
            copied,
            copied,
            block,
            copied,
            block,
            copied,
        ),
        out_specs=(
            rows,
            rows,
            block,
            copied,
            copied,
            copied,
            copied,
            block,
            copied,
            block,
            copied,
            block,
            copied,
            copied,
            copied,
            block,
            copied,
            copied,
            block,
            copied,
            copied,
            copied,
            block,
            copied,
            block,
            copied,
        ),
        check_vma=False,
    )
```

```python
import functools

import jax
import jax.numpy as jnp
from jax import lax
from jax.experimental import pallas as pl
from jax.experimental.pallas import tpu as pltpu
from jax.sharding import PartitionSpec as P

D = 512
HEADS = 16
HD = 32
FF = 2048
CIN = 256
G = 4
NL = 256
IN_G = 512
SEGS = 4
QT = 32
PACK = 256
TILES = NL // QT
SELF_GROUPS = 2
SELF_ROWS = SELF_GROUPS * NL
CROSS_GROUPS = 4
LAT_STEP = CROSS_GROUPS * NL
IN_STEP = CROSS_GROUPS * IN_G
UNITS = 4
WIDTHS = (128, 192, 256, 384, 512)

F32 = jnp.float32
BF16 = jnp.bfloat16
NEG_FILL = -1e30
EPSILON = 1e-05
SCALE = HD**-0.5
LOG2E = 1.4426950408889634
SCALE2 = SCALE * LOG2E
VMEM_BYTES = 60 * 1024 * 1024

TAIL_RATE = 0.28
TAIL_POLY = (
    0.1165209849818009,
    0.06749547174407416,
    0.2689133347091787,
    -0.23699737809142182,
    0.38987640062523105,
    -0.10580882324798475,
)

ROW_QGAIN, ROW_QSHIFT, ROW_SOURCE, ROW_QBIAS, ROW_VBIAS = range(5)
ROW_UBIAS, ROW_COBIAS, ROW_SGAIN, ROW_SSHIFT, ROW_SQBIAS = 8, 12, 13, 14, 15
ROW_SVBIAS, ROW_SOBIAS, ROW_FGAIN, ROW_FSHIFT, ROW_DBIAS = 16, 17, 18, 19, 20
VEC_ROWS = 24
CROSS_VECS = 8
MIDDLE_VECS = VEC_ROWS - CROSS_VECS

CHUNKS = 16
HALVES = 2
CROSS_MATS = ((G * NL, D), (D, D), (CIN, 2 * D))
MIDDLE_MATS = ((D, 3 * D), (D, D), (D, FF), (FF, D), (D, D))


def slab_place(mats, at):
    sizes = [rows // CHUNKS * (columns // (HALVES * PACK)) for rows, columns in mats]
    return sum(sizes[:at]), mats[at][0] // CHUNKS, sum(sizes)


LATENT, WQ, WKV = (slab_place(CROSS_MATS, at)[:2] for at in range(3))
WPROJ, WSO, WUP, WDN, WO = (slab_place(MIDDLE_MATS, at)[:2] for at in range(5))
CROSS_SLAB = slab_place(CROSS_MATS, 0)[2]
MIDDLE_SLAB = slab_place(MIDDLE_MATS, 0)[2]


def dot_plain(left, right):
    return lax.dot_general(left, right, (((1,), (0,)), ((), ())), preferred_element_type=F32)


def dot_first(left, right):
    return lax.dot_general(left, right, (((0,), (0,)), ((), ())), preferred_element_type=F32)


def dot_last(left, right):
    return lax.dot_general(left, right, (((1,), (1,)), ((), ())), preferred_element_type=F32)


def over_rows(total, chunk, body):
    def step(index, carry):
        body(pl.ds(pl.multiple_of(index * chunk, chunk), chunk))
        return carry

    lax.fori_loop(0, total // chunk, step, 0, unroll=8)


def norm_forward(rows, gain, shift):
    centered = rows - jnp.mean(rows, -1, keepdims=True)
    rscale = lax.rsqrt(jnp.mean(centered * centered, -1, keepdims=True) + EPSILON)
    normed = centered * rscale
    return normed * gain + shift, normed, rscale


def norm_backward(grad, normed, rscale, gain):
    dnormed = grad * gain
    return rscale * (
        dnormed
        - jnp.mean(dnormed, -1, keepdims=True)
        - normed * jnp.mean(dnormed * normed, -1, keepdims=True)
    )


def column_sum(rows):
    return jnp.sum(rows, 0, keepdims=True)


def gelu_pair(hidden):
    size = jnp.abs(hidden)
    ratio = 1.0 / (1.0 + TAIL_RATE * size)
    bell = jnp.exp2(hidden * hidden * (-0.5 * LOG2E))
    poly = TAIL_POLY[-1] * ratio
    for coefficient in TAIL_POLY[-2::-1]:
        poly = (poly + coefficient) * ratio
    tail = poly * bell
    cdf = jnp.where(hidden >= 0.0, 1.0 - tail, tail)
    return hidden * cdf, cdf + hidden * bell * 0.3989422804014327


def fill_block_mask(mask_ref):
    row_head = lax.broadcasted_iota(jnp.int32, (PACK, PACK), 0) // QT
    lane_head = lax.broadcasted_iota(jnp.int32, (PACK, PACK), 1) // HD
    mask_ref[...] = jnp.where(row_head == lane_head, 1.0, 0.0).astype(BF16)


def block_diagonal(rows, mask):
    return jnp.concatenate([rows] * (PACK // QT), 0) * mask


def take_diagonal(full):
    lane = lax.broadcasted_iota(jnp.int32, (QT, 128), 1)
    columns = []
    for half in range(2):
        base = 128 * half
        picked = full[base : base + QT, base : base + 128]
        for head in range(1, 4):
            row = base + QT * head
            picked = jnp.where(
                lane >= HD * head, full[row : row + QT, base : base + 128], picked
            )
        columns.append(picked)
    return jnp.concatenate(columns, 1)


def segment_at(cuts, place):
    return sum((place >= cut).astype(jnp.int32) for cut in cuts)


def pick(index, values):
    result = values[0]
    for at in range(1, len(values)):
        result = jnp.where(index == at, values[at], result)
    return result


def in_widths(plan_ref, step, body):
    first = CROSS_GROUPS * TILES

    for at, width in enumerate(WIDTHS):

        def batch_body(batch, carry, width=width):
            body(batch, width)
            return carry

        lax.fori_loop(plan_ref[step, first + at], plan_ref[step, first + at + 1], batch_body, 0)


def query_segments(query_cuts, tile):
    lane = lax.broadcasted_iota(jnp.int32, (1, PACK), 1) % QT
    return segment_at(query_cuts, tile * QT + lane)


def allowed_pairs(key_seg, query_seg):
    return jnp.concatenate([key_seg, key_seg], 1) == query_seg


def softmax_rows(scores, allowed):
    scores = jnp.where(allowed, scores, NEG_FILL)
    top = jnp.max(scores, 0, keepdims=True)
    powers = jnp.exp2((scores - top) * SCALE2)
    total = jnp.sum(powers, 0, keepdims=True)
    return (powers * (1.0 / total)).astype(BF16), top * SCALE2 + jnp.log2(total)


def score_grads(probs, dprobs):
    weighted = probs * dprobs
    delta = jnp.sum(weighted, 0, keepdims=True)
    return (weighted - probs * delta).astype(BF16)


def half(part):
    return slice(PACK * part, PACK * part + PACK)


def slab_part(slab_ref, place, side, piece):
    offset, rows = place
    part = slab_ref[:, side, offset + piece * rows : offset + piece * rows + rows, :]
    return part.reshape(CHUNKS * rows, PACK)


def slab_matrix(slab_ref, place, pieces):
    return jnp.concatenate(
        [
            slab_part(slab_ref, place, piece // (pieces // HALVES), piece % (pieces // HALVES))
            for piece in range(pieces)
        ],
        1,
    )


def store_halves(side, keep_ref, send_ref, place, matrix):
    offset, rows = place
    pieces = matrix.shape[1] // PACK
    inner = pieces // HALVES

    def store(refs):
        for piece in range(pieces):
            start = offset + piece % inner * rows
            part = matrix[:, piece * PACK : piece * PACK + PACK].astype(BF16)
            refs[piece // inner][:, start : start + rows, :] = part.reshape(CHUNKS, rows, PACK)

    @pl.when(side == 0)
    def _():
        store((keep_ref, send_ref))

    @pl.when(side != 0)
    def _():
        store((send_ref, keep_ref))


def latent_cuts(cuts_ref, group):
    return [cuts_ref[group, 4 + at] for at in range(SEGS - 1)]


def fill_cross_segments(seg_ref, cuts_ref, step):
    place = lax.broadcasted_iota(jnp.int32, (IN_G, 128), 0)
    for member in range(CROSS_GROUPS):
        key_cuts = [cuts_ref[step * CROSS_GROUPS + member, at] for at in range(SEGS - 1)]
        seg_ref[member * IN_G : member * IN_G + IN_G, :] = segment_at(key_cuts, place)


def cross_units(plan_ref, cuts_ref, seg_ref, step, batch, width):
    units = []
    for at in range(UNITS):
        packed = plan_ref[step, batch * UNITS + at]
        slot = packed // 1024
        start = pl.multiple_of(jnp.minimum(packed % 1024, IN_G - width), 16)
        member = slot // TILES
        tile = slot % TILES
        keys = pl.ds(pl.multiple_of(member * IN_G + start, 16), width)
        cuts = latent_cuts(cuts_ref, step * CROSS_GROUPS + member)
        allowed = allowed_pairs(seg_ref[keys, :], query_segments(cuts, tile))
        units.append((slot, pl.ds(pl.multiple_of(slot * QT, QT), QT), keys, allowed))
    return units


def plan_tiles(in_cuts, lat_cuts):
    groups = in_cuts.shape[0]
    tile = jnp.arange(TILES, dtype=jnp.int32) * QT
    first = jnp.sum(tile[None, :, None] >= lat_cuts[:, None, :], -1, dtype=jnp.int32)
    last = jnp.sum(tile[None, :, None] + (QT - 1) >= lat_cuts[:, None, :], -1, dtype=jnp.int32)
    starts = jnp.concatenate([jnp.zeros((groups, 1), jnp.int32), in_cuts], 1)
    ends = jnp.concatenate([in_cuts, jnp.full((groups, 1), IN_G, jnp.int32)], 1)
    segment = jnp.arange(SEGS, dtype=jnp.int32)
    low = jnp.sum(jnp.where(first[..., None] == segment, starts[:, None, :], 0), -1) // 16 * 16
    high = jnp.sum(jnp.where(last[..., None] == segment, ends[:, None, :], 0), -1)
    count = CROSS_GROUPS * TILES
    low = low.reshape(-1, count)
    needed = high.reshape(-1, count) - low
    slot = jnp.arange(count, dtype=jnp.int32)
    earlier = slot[:, None] < slot[None, :]
    mine, other = needed[:, None, :], needed[:, :, None]
    rank = jnp.sum((other < mine) | ((other == mine) & earlier), 1, dtype=jnp.int32)
    place = rank[:, None, :] == slot[:, None]
    packed = jnp.sum(jnp.where(place, (slot * 1024 + low)[:, None, :], 0), -1)
    batches = jnp.arange(count // UNITS, dtype=jnp.int32)[:, None]
    inside = rank[:, None, :] // UNITS == batches
    widest = jnp.max(jnp.where(inside, needed[:, None, :], 0), -1)
    widths = jnp.array((0,) + WIDTHS, jnp.int32)
    bounds = jnp.sum(widest[:, :, None] <= widths, 1, dtype=jnp.int32)
    return jnp.concatenate([packed, bounds], 1).astype(jnp.int32)


def cross_forward_kernel(
    cuts_ref,
    plan_ref,
    source_ref,
    slab_ref,
    vec_ref,
    mix_ref,
    kv_ref,
    lse_ref,
    query_ref,
    latent_ref,
    mask_ref,
    seg_ref,
):
    step = pl.program_id(0)

    @pl.when(step == 0)
    def _():
        fill_block_mask(mask_ref)
        latent = slab_matrix(slab_ref, LATENT, 2)
        latent_ref[...] = latent
        low, _, _ = norm_forward(
            latent.astype(F32),
            vec_ref[ROW_QGAIN : ROW_QGAIN + 1, :],
            vec_ref[ROW_QSHIFT : ROW_QSHIFT + 1, :],
        )
        query = dot_plain(low.astype(BF16), slab_matrix(slab_ref, WQ, 2))
        query_ref[...] = (query + vec_ref[ROW_QBIAS : ROW_QBIAS + 1, :]).astype(BF16)

    wkv = slab_matrix(slab_ref, WKV, 4)
    kv_ref[:, :D] = dot_plain(source_ref[...], wkv[:, :D]).astype(BF16)
    kv_ref[:, D:] = (
        dot_plain(source_ref[...], wkv[:, D:]) + vec_ref[ROW_VBIAS : ROW_VBIAS + 1, :]
    ).astype(BF16)

    fill_cross_segments(seg_ref, cuts_ref, step)

    def window(batch, width):
        units = cross_units(plan_ref, cuts_ref, seg_ref, step, batch, width)
        scores = [
            dot_last(
                kv_ref[keys, half(part)],
                block_diagonal(query_ref[rows, half(part)], mask_ref[...]),
            )
            for _, rows, keys, _ in units
            for part in range(2)
        ]
        probs = []
        for at, (slot, _, _, allowed) in enumerate(units):
            for part in range(2):
                low, lse = softmax_rows(scores[2 * at + part], allowed)
                probs.append(low)
                lse_ref[pl.ds(slot * 2 + part, 1), :] = lse
        for at, (_, rows, keys, _) in enumerate(units):
            for part in range(2):
                full = dot_first(probs[2 * at + part], kv_ref[keys, half(part + 2)])
                mix_ref[rows, half(part)] = take_diagonal(full).astype(BF16)

    in_widths(plan_ref, step, window)


def middle_kernel(
    cuts_ref,
    side_ref,
    cross_mix_ref,
    cot_ref,
    latent_ref,
    slab_ref,
    vec_ref,
    active_ref,
    after_self_ref,
    dcross_mix_ref,
    glat_ref,
    small_ref,
    keep_ref,
    send_ref,
    mask_ref,
    after_ref,
    hat1_ref,
    rs1_ref,
    low1_ref,
    triple_ref,
    probs_ref,
    mix_ref,
    res_ref,
    hat2_ref,
    rs2_ref,
    low2_ref,
    dtop_ref,
    dso_ref,
    dmix_ref,
    dtriple_ref,
    aproj_ref,
    aso_ref,
    aup_ref,
    adn_ref,
    ao_ref,
):
    step = pl.program_id(0)
    last = pl.num_programs(0) - 1

    def vec(row):
        return vec_ref[row : row + 1, :]

    def add_small(row, value):
        small_ref[row - CROSS_VECS : row - CROSS_VECS + 1, :] += value

    @pl.when(step == 0)
    def _():
        fill_block_mask(mask_ref)
        for ref in (glat_ref, small_ref, aproj_ref, aso_ref, aup_ref, adn_ref, ao_ref):
            ref[...] = jnp.zeros(ref.shape, ref.dtype)

    base = pl.multiple_of(step % (G // SELF_GROUPS) * SELF_ROWS, SELF_ROWS)
    after_ref[...] = (
        latent_ref[pl.ds(base, SELF_ROWS), :].astype(F32)
        + dot_plain(cross_mix_ref[...], slab_matrix(slab_ref, WO, 2))
        + vec(ROW_COBIAS)
    )

    def first_norm(rows):
        low, normed, rscale = norm_forward(after_ref[rows, :], vec(ROW_SGAIN), vec(ROW_SSHIFT))
        low1_ref[rows, :] = low.astype(BF16)
        hat1_ref[rows, :] = normed
        rs1_ref[rows, :] = rscale

    over_rows(SELF_ROWS, 64, first_norm)
    wproj = slab_matrix(slab_ref, WPROJ, 6)
    for block, bias in enumerate((ROW_SQBIAS, None, ROW_SVBIAS)):
        columns = slice(D * block, D * block + D)
        product = dot_plain(low1_ref[...], wproj[:, columns])
        if bias is not None:
            product = product + vec(bias)
        triple_ref[:, columns] = product.astype(BF16)

    units = [(member, part) for member in range(SELF_GROUPS) for part in range(2)]

    def group_rows(member):
        return slice(member * NL, member * NL + NL)

    def block_rows(ref, member, part):
        starts = range(member * NL, member * NL + NL, QT)
        return jnp.concatenate(
            [block_diagonal(ref[at : at + QT, half(part)], mask_ref[...]) for at in starts], 0
        )

    def unit_scores(member, part):
        keys = triple_ref[group_rows(member), half(part + 2)]
        return dot_last(block_rows(triple_ref, member, part), keys)

    ahead = unit_scores(*units[0])
    for at, (member, part) in enumerate(units):
        scores = ahead
        if at + 1 < len(units):
            ahead = unit_scores(*units[at + 1])
        cuts = latent_cuts(cuts_ref, step * SELF_GROUPS + member)
        key_seg = segment_at(cuts, lax.broadcasted_iota(jnp.int32, (QT, NL), 1))
        place = lax.broadcasted_iota(jnp.int32, (QT, NL), 0)
        probs = []
        for tile in range(TILES):
            allowed = segment_at(cuts, tile * QT + place) == key_seg
            block = scores[tile * PACK : tile * PACK + PACK].reshape(PACK // QT, QT, NL)
            block = jnp.where(allowed[None], block, NEG_FILL)
            top = jnp.max(block, 2, keepdims=True)
            powers = jnp.exp2((block - top) * SCALE2)
            total = jnp.sum(powers, 2, keepdims=True)
            probs.append((powers * (1.0 / total)).reshape(PACK, NL).astype(BF16))
        probs = jnp.concatenate(probs, 0)
        probs_ref[member * 2 + part] = probs
        full = dot_plain(probs, triple_ref[group_rows(member), half(part + 4)])
        for tile in range(TILES):
            rows = slice(member * NL + tile * QT, member * NL + tile * QT + QT)
            mixed = take_diagonal(full[tile * PACK : tile * PACK + PACK])
            mix_ref[rows, half(part)] = mixed.astype(BF16)

    after_self_ref[...] = after_ref[...] + dot_plain(mix_ref[...], slab_matrix(slab_ref, WSO, 2)) + vec(ROW_SOBIAS)

    def second_norm(rows):
        low, normed, rscale = norm_forward(after_self_ref[rows, :], vec(ROW_FGAIN), vec(ROW_FSHIFT))
        low2_ref[rows, :] = low.astype(BF16)
        hat2_ref[rows, :] = normed
        rs2_ref[rows, :] = rscale

    over_rows(SELF_ROWS, 64, second_norm)
    dtop_ref[...] = jnp.zeros(dtop_ref.shape, F32)

    def feed_front(block):
        up = slab_part(slab_ref, WUP, *divmod(block, FF // PACK // HALVES))
        offset, height = WDN
        chunks = slice(block * PACK // height, (block + 1) * PACK // height)
        down = jnp.concatenate(
            [
                slab_ref[chunks, side, offset : offset + height, :].reshape(PACK, PACK)
                for side in range(HALVES)
            ],
            1,
        )
        row, column = divmod(block * PACK, D)
        bias = vec_ref[ROW_UBIAS + row : ROW_UBIAS + row + 1, column : column + PACK]
        hidden = dot_plain(low2_ref[...], up) + bias
        return up, down, hidden, dot_last(cot_ref[...], down)

    ahead = feed_front(0)
    for block in range(FF // PACK):
        up, down, hidden, dactive = ahead
        if block + 1 < FF // PACK:
            ahead = feed_front(block + 1)
        active, slope = gelu_pair(hidden)
        active = active.astype(BF16)
        dhidden = slope * dactive
        row, column = divmod(block * PACK, D)
        row += ROW_UBIAS - CROSS_VECS
        small_ref[row : row + 1, column : column + PACK] += column_sum(dhidden)
        dhidden = dhidden.astype(BF16)
        columns = slice(block * PACK, block * PACK + PACK)
        adn_ref[columns, :] += dot_first(active, cot_ref[...])
        aup_ref[:, columns] += dot_first(low2_ref[...], dhidden)
        active_ref[:, columns] = active
        dtop_ref[...] += dot_last(dhidden, up)

    def after_feed(rows):
        dtop = dtop_ref[rows, :]
        normed = hat2_ref[rows, :]
        cot = cot_ref[rows, :].astype(F32)
        dafter = cot + norm_backward(dtop, normed, rs2_ref[rows, :], vec(ROW_FGAIN))
        dlow = dafter.astype(BF16)
        res_ref[rows, :] = dafter
        dso_ref[rows, :] = dlow
        add_small(ROW_FGAIN, column_sum(dtop * normed))
        add_small(ROW_FSHIFT, column_sum(dtop))
        add_small(ROW_DBIAS, column_sum(cot))
        add_small(ROW_SOBIAS, column_sum(dlow.astype(F32)))

    over_rows(SELF_ROWS, 64, after_feed)
    aso_ref[...] += dot_first(mix_ref[...], dso_ref[...])
    dmix_ref[...] = dot_last(dso_ref[...], slab_matrix(slab_ref, WSO, 2)).astype(BF16)

    def unit_dprobs(member, part):
        grads = block_rows(dmix_ref, member, part)
        values = triple_ref[group_rows(member), half(part + 4)]
        return grads, dot_last(grads, values)

    ahead = unit_dprobs(*units[0])
    for at, (member, part) in enumerate(units):
        grads, dprobs = ahead
        if at + 1 < len(units):
            ahead = unit_dprobs(*units[at + 1])
        group = group_rows(member)
        probs = probs_ref[member * 2 + part]
        dtriple_ref[group, half(part + 4)] = dot_first(probs, grads).astype(BF16)
        dscores = []
        for tile in range(TILES):
            rows = slice(tile * PACK, tile * PACK + PACK)
            block = probs[rows].astype(F32)
            weighted = block * dprobs[rows]
            delta = jnp.sum(weighted, 1, keepdims=True)
            dscores.append((weighted - block * delta).astype(BF16))
        dscores = jnp.concatenate(dscores, 0)
        dkeys = dot_first(dscores, block_rows(triple_ref, member, part))
        dtriple_ref[group, half(part + 2)] = (dkeys * SCALE).astype(BF16)
        full = dot_plain(dscores, triple_ref[group, half(part + 2)])
        for tile in range(TILES):
            rows = slice(member * NL + tile * QT, member * NL + tile * QT + QT)
            dquery = take_diagonal(full[tile * PACK : tile * PACK + PACK])
            dtriple_ref[rows, half(part)] = (dquery * SCALE).astype(BF16)
    for block in range(3):
        columns = slice(D * block, D * block + D)
        aproj_ref[:, columns] += dot_first(low1_ref[...], dtriple_ref[:, columns])
    add_small(ROW_SQBIAS, column_sum(dtriple_ref[:, :D].astype(F32)))
    add_small(ROW_SVBIAS, column_sum(dtriple_ref[:, 2 * D :].astype(F32)))
    dtop_ref[...] = dot_last(dtriple_ref[...], slab_matrix(slab_ref, WPROJ, 6))

    def after_self(rows):
        dmid = dtop_ref[rows, :]
        normed = hat1_ref[rows, :]
        dafter = res_ref[rows, :] + norm_backward(dmid, normed, rs1_ref[rows, :], vec(ROW_SGAIN))
        dlow = dafter.astype(BF16)
        dso_ref[rows, :] = dlow
        glat_ref[pl.ds(pl.multiple_of(base + rows.start, 64), rows.size), :] += dafter
        add_small(ROW_SGAIN, column_sum(dmid * normed))
        add_small(ROW_SSHIFT, column_sum(dmid))
        add_small(ROW_COBIAS, column_sum(dlow.astype(F32)))

    over_rows(SELF_ROWS, 64, after_self)
    ao_ref[...] += dot_first(cross_mix_ref[...], dso_ref[...])
    dcross_mix_ref[...] = dot_last(dso_ref[...], slab_matrix(slab_ref, WO, 2)).astype(BF16)

    @pl.when(step == last)
    def _():
        side = side_ref[0]
        store_halves(side, keep_ref, send_ref, WPROJ, aproj_ref[...])
        store_halves(side, keep_ref, send_ref, WSO, aso_ref[...])
        store_halves(side, keep_ref, send_ref, WUP, aup_ref[...])
        store_halves(side, keep_ref, send_ref, WDN, adn_ref[...])
        store_halves(side, keep_ref, send_ref, WO, ao_ref[...])


def row_dot(rows, matrix):
    high = rows.astype(BF16)
    low = (rows - high.astype(F32)).astype(BF16)
    return dot_last(high, matrix) + dot_last(low, matrix)


def row_sums(matrix):
    high = matrix.astype(BF16)
    low = (matrix - high.astype(F32)).astype(BF16)
    ones = jnp.ones((8, matrix.shape[1]), BF16)
    return (dot_last(ones, high) + dot_last(ones, low))[:1]


VECTOR_PLACES = (
    (ROW_QGAIN, 0),
    (ROW_QSHIFT, 0),
    (ROW_SOURCE, 0),
    (ROW_SOURCE, CIN),
    (ROW_QBIAS, 0),
    (ROW_VBIAS, 0),
    (ROW_COBIAS, 0),
    (ROW_SGAIN, 0),
    (ROW_SSHIFT, 0),
    (ROW_SQBIAS, 0),
    (ROW_SVBIAS, 0),
    (ROW_SOBIAS, 0),
    (ROW_FGAIN, 0),
    (ROW_FSHIFT, 0),
    (ROW_UBIAS, 0),
    (ROW_DBIAS, 0),
)


def cross_backward_kernel(
    cuts_ref,
    plan_ref,
    side_ref,
    source_ref,
    kv_ref,
    lse_ref,
    dmix_ref,
    query_ref,
    glat_ref,
    slab_ref,
    vec_ref,
    dkv_ref,
    keep_ref,
    send_ref,
    small_ref,
    mask_ref,
    seg_ref,
    dkey_ref,
    dvalue_ref,
    dquery_ref,
    akv_ref,
    dsum_ref,
):
    step = pl.program_id(0)
    last = pl.num_programs(0) - 1

    def vec(row):
        return vec_ref[row : row + 1, :]

    def add_small(row, value):
        small_ref[row : row + 1, :] += value

    def add_row(ref, value):
        ref[...] += value

    @pl.when(step == 0)
    def _():
        fill_block_mask(mask_ref)
        for ref in (small_ref, dquery_ref, akv_ref, dsum_ref):
            ref[...] = jnp.zeros(ref.shape, ref.dtype)

    fill_cross_segments(seg_ref, cuts_ref, step)
    dkey_ref[...] = jnp.zeros(dkey_ref.shape, F32)
    dvalue_ref[...] = jnp.zeros(dvalue_ref.shape, F32)

    def window(batch, width):
        units = cross_units(plan_ref, cuts_ref, seg_ref, step, batch, width)
        work = []
        for slot, rows, keys, allowed in units:
            for part in range(2):
                queries = block_diagonal(query_ref[rows, half(part)], mask_ref[...])
                grads = block_diagonal(dmix_ref[rows, half(part)], mask_ref[...])
                scores = dot_last(kv_ref[keys, half(part)], queries)
                dprobs = dot_last(kv_ref[keys, half(part + 2)], grads)
                work.append((slot, rows, keys, allowed, part, queries, grads, scores, dprobs))
        ready = []
        for slot, rows, keys, allowed, part, queries, grads, scores, dprobs in work:
            lse = lse_ref[pl.ds(slot * 2 + part, 1), :]
            probs = jnp.exp2(jnp.where(allowed, scores * SCALE2 - lse, NEG_FILL))
            dscores = score_grads(probs, dprobs)
            ready.append((rows, keys, part, queries, grads, probs.astype(BF16), dscores))
        for rows, keys, part, queries, grads, probs, dscores in ready:
            dvalue_ref[keys, half(part)] += dot_plain(probs, grads)
            dkey_ref[keys, half(part)] += dot_plain(dscores, queries)
            dquery_ref[rows, half(part)] += take_diagonal(
                dot_first(dscores, kv_ref[keys, half(part)])
            )

    in_widths(plan_ref, step, window)
    dkv_ref[:, :D] = (dkey_ref[...] * SCALE).astype(BF16)
    dkv_ref[:, D:] = dvalue_ref[...].astype(BF16)

    for part in range(2):
        columns = slice(D * part, D * part + D)
        akv_ref[:, columns] += dot_first(source_ref[...], dkv_ref[:, columns])
    over_rows(IN_STEP, 256, lambda rows: add_row(dsum_ref, column_sum(dkv_ref[rows, :].astype(F32))))

    @pl.when(step == last)
    def _():
        side = side_ref[0]
        store_halves(side, keep_ref, send_ref, WKV, akv_ref[...])
        wkv = slab_matrix(slab_ref, WKV, 4)
        sums = dsum_ref[...]
        add_small(ROW_VBIAS, sums[:, D:])
        shift_grad = row_dot(jnp.broadcast_to(sums, (8, 2 * D)), wkv)[:1]
        product = wkv.astype(F32) * akv_ref[...]
        both = row_sums(product)
        gain = vec_ref[ROW_SOURCE : ROW_SOURCE + 1, :CIN]
        shift = vec_ref[ROW_SOURCE : ROW_SOURCE + 1, CIN:]
        small_ref[ROW_SOURCE : ROW_SOURCE + 1, :CIN] = (both - shift * shift_grad) / gain
        small_ref[ROW_SOURCE : ROW_SOURCE + 1, CIN:] = shift_grad
        low, normed, rscale = norm_forward(
            slab_matrix(slab_ref, LATENT, 2).astype(F32), vec(ROW_QGAIN), vec(ROW_QSHIFT)
        )
        dquery = (dquery_ref[...] * SCALE).astype(BF16)
        store_halves(side, keep_ref, send_ref, WQ, dot_first(low.astype(BF16), dquery))
        add_small(ROW_QBIAS, column_sum(dquery.astype(F32)))
        dnorm = dot_last(dquery, slab_matrix(slab_ref, WQ, 2))
        add_small(ROW_QGAIN, column_sum(dnorm * normed))
        add_small(ROW_QSHIFT, column_sum(dnorm))
        total = glat_ref[...] + norm_backward(dnorm, normed, rscale, vec(ROW_QGAIN))
        store_halves(side, keep_ref, send_ref, LATENT, total)


def output_kernel(active_ref, after_self_ref, slab_ref, vec_ref, out_ref):
    total = after_self_ref[...] + dot_plain(active_ref[...], slab_matrix(slab_ref, WDN, 2))
    out_ref[...] = (total + vec_ref[ROW_DBIAS : ROW_DBIAS + 1, :]).astype(BF16)


def source_kernel(inputs_ref, dkv_ref, slab_ref, vec_ref, dinput_ref):
    gain = vec_ref[ROW_SOURCE : ROW_SOURCE + 1, :CIN]
    shift = vec_ref[ROW_SOURCE : ROW_SOURCE + 1, CIN:]
    wkv = slab_matrix(slab_ref, WKV, 4)

    def source_back(rows):
        dsource = dot_last(dkv_ref[rows, :], wkv)
        _, normed, rscale = norm_forward(inputs_ref[rows, :].astype(F32), gain, shift)
        dinput_ref[rows, :] = norm_backward(dsource, normed, rscale, gain)

    over_rows(IN_STEP, 256, source_back)


def pack_kernel(*refs):
    cross, middle = refs[: len(CROSS_MATS)], refs[len(CROSS_MATS) : -2]
    copies_ref, packed_ref = refs[-2:]
    for targets, shards in (((copies_ref, True), cross), ((packed_ref, False), middle)):
        target_ref, copied = targets
        start = 0
        for shard in shards:
            rows, columns = shard.shape
            for column in range(0, columns, PACK):
                part = shard[:, column : column + PACK]
                if copied:
                    part = jnp.broadcast_to(part, (CHUNKS, rows, PACK))
                    target_ref[:, start : start + rows, :] = part
                else:
                    target_ref[start : start + rows, :] = part
                start += rows


def combine_kernel(keep_ref, sent_ref, small_ref, small_sent_ref, out_ref):
    total = keep_ref[...].astype(F32) + sent_ref[...].astype(F32)
    out_ref[:, :CROSS_SLAB, :] = total.astype(BF16)
    small = small_ref[...] + small_sent_ref[...]
    small = jnp.concatenate([small[:, :PACK], small[:, PACK:]], 0)
    high = small.astype(BF16)
    low = (small - high.astype(F32)).astype(BF16)
    rows = 2 * CROSS_VECS
    for at, part in enumerate((high, low)):
        start = CROSS_SLAB + at * rows
        out_ref[:, start : start + rows, :] = jnp.broadcast_to(part, (CHUNKS, rows, PACK))


def finish_kernel(parts_ref, middle_ref, small_ref, *outs):
    mats, vectors = outs[: len(CROSS_MATS) + len(MIDDLE_MATS)], outs[-16:]
    total = parts_ref[0].astype(F32)
    for at in range(1, CHUNKS):
        total = total + parts_ref[at].astype(F32)
    middle = middle_ref[...].astype(F32)
    for source, shards in ((total, mats[: len(CROSS_MATS)]), (middle, mats[len(CROSS_MATS) :])):
        start = 0
        for shard in shards:
            rows, columns = shard.shape
            for column in range(0, columns, PACK):
                shard[:, column : column + PACK] = source[start : start + rows]
                start += rows
    rows = 2 * CROSS_VECS
    small = total[CROSS_SLAB : CROSS_SLAB + rows] + total[CROSS_SLAB + rows :]
    small = jnp.concatenate([small[:CROSS_VECS], small[CROSS_VECS:]], 1)
    write_vectors(jnp.concatenate([small, jnp.sum(small_ref[...], 0)], 0), vectors)


def write_vectors(rows, vectors):
    for ref, (row, start) in zip(vectors, VECTOR_PLACES):
        size = ref.shape[-1]
        taken = [
            rows[row + at : row + at + 1, start : start + min(size, D)]
            for at in range(max(1, size // D))
        ]
        ref[...] = jnp.concatenate(taken, 1)


def rows_spec(rows, columns):
    return pl.BlockSpec((rows, columns), lambda step, *scalars: (step, 0))


def whole_spec(rows, columns):
    return pl.BlockSpec(
        (rows, columns), lambda step, *scalars: (0, 0), pipeline_mode=pl.Buffered(1)
    )


def kernel_call(kernel, scalars, steps, in_specs, out_specs, out_shape, scratch, flops):
    return pl.pallas_call(
        kernel,
        grid_spec=pltpu.PrefetchScalarGridSpec(
            num_scalar_prefetch=scalars,
            grid=(steps,),
            in_specs=in_specs,
            out_specs=out_specs,
            scratch_shapes=scratch,
        ),
        out_shape=out_shape,
        compiler_params=pltpu.CompilerParams(
            vmem_limit_bytes=VMEM_BYTES, dimension_semantics=("arbitrary",)
        ),
        cost_estimate=pl.CostEstimate(
            flops=flops, bytes_accessed=100 * 2**20, transcendentals=0
        ),
    )


def slab_spec(rows):
    return pl.BlockSpec(
        (CHUNKS, HALVES, rows, PACK),
        lambda step, *scalars: (0, 0, 0, 0),
        pipeline_mode=pl.Buffered(1),
    )


def slab_shape(rows):
    return jax.ShapeDtypeStruct((CHUNKS, HALVES, rows, PACK), BF16)


def gather_whole(shards):
    parts = []
    for shard in shards:
        full = lax.all_gather(
            lax.all_gather(shard, "narrow", axis=1, tiled=True), "wide", axis=0, tiled=True
        )
        rows, columns = full.shape
        split = full.reshape(CHUNKS, rows // CHUNKS, HALVES, columns // (HALVES * PACK), PACK)
        parts.append(split.transpose(0, 2, 3, 1, 4).reshape(CHUNKS, HALVES, -1, PACK))
    return jnp.concatenate(parts, 2)


def scatter_whole(slab, mats):
    shards = []
    start = 0
    for rows, columns in mats:
        height = rows // CHUNKS
        pieces = columns // (HALVES * PACK)
        part = slab[:, :, start : start + height * pieces]
        start += height * pieces
        part = part.reshape(CHUNKS, HALVES, pieces, height, PACK).transpose(0, 3, 1, 2, 4)
        total = lax.psum_scatter(
            part.reshape(rows, columns), "wide", scatter_dimension=0, tiled=True
        )
        total = lax.psum_scatter(total, "narrow", scatter_dimension=1, tiled=True)
        shards.append(total.astype(F32))
    return shards


SWAP = ((0, 1), (1, 0))


def simple_call(kernel, out_shape):
    return pl.pallas_call(
        kernel,
        out_shape=out_shape,
        compiler_params=pltpu.CompilerParams(vmem_limit_bytes=VMEM_BYTES),
    )


def half_shape(rows):
    return jax.ShapeDtypeStruct((CHUNKS, rows, PACK), BF16)


def half_spec(rows):
    return pl.BlockSpec(
        (CHUNKS, rows, PACK), lambda step, *scalars: (0, 0, 0), pipeline_mode=pl.Buffered(1)
    )


def gather_soon(copies):
    mine = lax.all_to_all(copies, "wide", 0, 0)
    other = lax.ppermute(mine, "narrow", SWAP)
    first = lax.axis_index("narrow") == 0
    return jnp.stack([jnp.where(first, mine, other), jnp.where(first, other, mine)], 1)


def gather_later(packed):
    full = lax.all_gather(packed, ("wide", "narrow"), axis=0)
    return full.reshape((CHUNKS, HALVES) + packed.shape)


def scatter_later(keep, send):
    sent = lax.ppermute(send, "narrow", SWAP)
    total = (keep.astype(F32) + sent.astype(F32)).astype(BF16)
    return lax.psum_scatter(total, "wide", scatter_dimension=0)


def scatter_soon(keep, send, small):
    sent = lax.ppermute(send, "narrow", SWAP)
    small_sent = lax.ppermute(small, "narrow", SWAP)
    rows = CROSS_SLAB + 4 * CROSS_VECS
    combined = simple_call(combine_kernel, half_shape(rows))(keep, sent, small, small_sent)
    return lax.all_to_all(combined, "wide", 0, 0)


def shape(rows, columns, dtype):
    return jax.ShapeDtypeStruct((rows, columns), dtype)


def local(
    wide,
    narrow,
    inputs,
    input_segments,
    latent_segments,
    cotangent,
    latent_array,
    query_gain,
    query_shift,
    source_gain,
    source_shift,
    cross_query,
    cross_qbias,
    cross_keyval,
    cross_vbias,
    cross_output,
    cross_obias,
    self_gain,
    self_shift,
    self_project,
    self_qbias,
    self_vbias,
    self_output,
    self_obias,
    feed_gain,
    feed_shift,
    feed_upward,
    feed_ubias,
    feed_downward,
    feed_dbias,
):
    lat_rows = cotangent.shape[0]
    in_rows = inputs.shape[0]
    groups = lat_rows // NL
    steps = groups // CROSS_GROUPS
    self_steps = groups // SELF_GROUPS

    vectors = jnp.concatenate(
        [
            query_gain,
            query_shift,
            source_gain,
            source_shift,
            cross_qbias,
            cross_vbias,
            jnp.zeros(((ROW_UBIAS - ROW_VBIAS - 1) * D,), BF16),
            feed_ubias,
            cross_obias,
            self_gain,
            self_shift,
            self_qbias,
            self_vbias,
            self_obias,
            feed_gain,
            feed_shift,
            feed_dbias,
            jnp.zeros(((VEC_ROWS - ROW_DBIAS - 1) * D,), BF16),
        ]
    )
    vectors = vectors.astype(F32).reshape(VEC_ROWS, D)
    marks = jnp.arange(1, SEGS, dtype=jnp.int32)
    in_cuts = jnp.sum(input_segments.reshape(groups, IN_G, 1) < marks, 1, dtype=jnp.int32)
    lat_cuts = jnp.sum(latent_segments.reshape(groups, NL, 1) < marks, 1, dtype=jnp.int32)
    blank = jnp.zeros((groups, 1), jnp.int32)
    cuts = jnp.concatenate([in_cuts, blank, lat_cuts, blank], 1)
    plan = plan_tiles(in_cuts, lat_cuts)

    source_low, _, _ = norm_forward(
        inputs.astype(F32), source_gain.astype(F32), source_shift.astype(F32)
    )
    source_low = source_low.astype(BF16)

    cross_shards = (latent_array, cross_query, cross_keyval)
    middle_shards = (self_project, self_output, feed_upward, feed_downward, cross_output)
    packed = (wide, narrow) == (CHUNKS, HALVES)
    if packed:
        copies, middle_packed = simple_call(
            pack_kernel, [half_shape(CROSS_SLAB), shape(MIDDLE_SLAB, PACK, BF16)]
        )(*cross_shards, *middle_shards)
        cross_slab = gather_soon(copies)
        middle_slab = gather_later(middle_packed)
        side = lax.axis_index("narrow").astype(jnp.int32).reshape(1)
    else:
        cross_slab = gather_whole(cross_shards)
        middle_slab = gather_whole(middle_shards)
        side = jnp.zeros((1,), jnp.int32)

    vec_spec = whole_spec(VEC_ROWS, D)
    lse_rows = CROSS_GROUPS * TILES * 2
    cross_mix, keyval, lse, query, latent_full = kernel_call(
        cross_forward_kernel,
        2,
        steps,
        [rows_spec(IN_STEP, CIN), slab_spec(CROSS_SLAB), vec_spec],
        [
            rows_spec(LAT_STEP, D),
            rows_spec(IN_STEP, 2 * D),
            rows_spec(lse_rows, PACK),
            whole_spec(G * NL, D),
            whole_spec(G * NL, D),
        ],
        [
            shape(lat_rows, D, BF16),
            shape(in_rows, 2 * D, BF16),
            shape(steps * lse_rows, PACK, F32),
            shape(G * NL, D, BF16),
            shape(G * NL, D, BF16),
        ],
        [
            pltpu.VMEM((PACK, PACK), BF16),
            pltpu.VMEM((IN_STEP, 128), jnp.int32),
        ],
        60 * 10**9,
    )(cuts, plan, source_low, cross_slab, vectors)

    active, after_self, dcross_mix, glat, middle_small, middle_keep, middle_send = kernel_call(
        middle_kernel,
        2,
        self_steps,
        [
            rows_spec(SELF_ROWS, D),
            rows_spec(SELF_ROWS, D),
            whole_spec(G * NL, D),
            slab_spec(MIDDLE_SLAB),
            vec_spec,
        ],
        [
            rows_spec(SELF_ROWS, FF),
            rows_spec(SELF_ROWS, D),
            rows_spec(SELF_ROWS, D),
            whole_spec(G * NL, D),
            whole_spec(MIDDLE_VECS, D),
            half_spec(MIDDLE_SLAB),
            half_spec(MIDDLE_SLAB),
        ],
        [
            shape(lat_rows, FF, BF16),
            shape(lat_rows, D, F32),
            shape(lat_rows, D, BF16),
            shape(G * NL, D, F32),
            shape(MIDDLE_VECS, D, F32),
            half_shape(MIDDLE_SLAB),
            half_shape(MIDDLE_SLAB),
        ],
        [
            pltpu.VMEM((PACK, PACK), BF16),
            pltpu.VMEM((SELF_ROWS, D), F32),
            pltpu.VMEM((SELF_ROWS, D), F32),
            pltpu.VMEM((SELF_ROWS, 1), F32),
            pltpu.VMEM((SELF_ROWS, D), BF16),
            pltpu.VMEM((SELF_ROWS, 3 * D), BF16),
            pltpu.VMEM((SELF_GROUPS * 2, TILES * PACK, NL), BF16),
            pltpu.VMEM((SELF_ROWS, D), BF16),
            pltpu.VMEM((SELF_ROWS, D), F32),
            pltpu.VMEM((SELF_ROWS, D), F32),
            pltpu.VMEM((SELF_ROWS, 1), F32),
            pltpu.VMEM((SELF_ROWS, D), BF16),
            pltpu.VMEM((SELF_ROWS, D), F32),
            pltpu.VMEM((SELF_ROWS, D), BF16),
            pltpu.VMEM((SELF_ROWS, D), BF16),
            pltpu.VMEM((SELF_ROWS, 3 * D), BF16),
            pltpu.VMEM((D, 3 * D), F32),
            pltpu.VMEM((D, D), F32),
            pltpu.VMEM((D, FF), F32),
            pltpu.VMEM((FF, D), F32),
            pltpu.VMEM((D, D), F32),
        ],
        250 * 10**9,
    )(cuts, side, cross_mix, cotangent, latent_full, middle_slab, vectors)

    dkeyval, cross_keep, cross_send, cross_small = kernel_call(
        cross_backward_kernel,
        3,
        steps,
        [
            rows_spec(IN_STEP, CIN),
            rows_spec(IN_STEP, 2 * D),
            rows_spec(lse_rows, PACK),
            rows_spec(LAT_STEP, D),
            whole_spec(G * NL, D),
            whole_spec(G * NL, D),
            slab_spec(CROSS_SLAB),
            vec_spec,
        ],
        [
            rows_spec(IN_STEP, 2 * D),
            half_spec(CROSS_SLAB),
            half_spec(CROSS_SLAB),
            whole_spec(CROSS_VECS, D),
        ],
        [
            shape(in_rows, 2 * D, BF16),
            half_shape(CROSS_SLAB),
            half_shape(CROSS_SLAB),
            shape(CROSS_VECS, D, F32),
        ],
        [
            pltpu.VMEM((PACK, PACK), BF16),
            pltpu.VMEM((IN_STEP, 128), jnp.int32),
            pltpu.VMEM((IN_STEP, D), F32),
            pltpu.VMEM((IN_STEP, D), F32),
            pltpu.VMEM((G * NL, D), F32),
            pltpu.VMEM((CIN, 2 * D), F32),
            pltpu.VMEM((1, 2 * D), F32),
        ],
        100 * 10**9,
    )(cuts, plan, side, source_low, keyval, lse, dcross_mix, query, glat, cross_slab, vectors)

    late_vectors, _ = lax.optimization_barrier((vectors, cross_small))
    latents_out = kernel_call(
        output_kernel,
        0,
        steps,
        [
            rows_spec(LAT_STEP, FF),
            rows_spec(LAT_STEP, D),
            slab_spec(MIDDLE_SLAB),
            vec_spec,
        ],
        rows_spec(LAT_STEP, D),
        shape(lat_rows, D, BF16),
        [],
        13 * 10**9,
    )(active, after_self, middle_slab, late_vectors)

    dinput = kernel_call(
        source_kernel,
        0,
        steps,
        [rows_spec(IN_STEP, CIN), rows_spec(IN_STEP, 2 * D), slab_spec(CROSS_SLAB), vec_spec],
        rows_spec(IN_STEP, CIN),
        shape(in_rows, CIN, F32),
        [],
        20 * 10**9,
    )(inputs, dkeyval, cross_slab, vectors)

    axes = ("wide", "narrow")
    vector_sizes = [D, D, CIN, CIN] + [D] * 10 + [FF, D]
    if packed:
        middle_total = scatter_later(middle_keep, middle_send)
        small_all = lax.all_gather(middle_small, axes, axis=0)
        parts = scatter_soon(cross_keep, cross_send, cross_small)
        mats = [
            shape(rows // CHUNKS, columns // HALVES, F32)
            for rows, columns in CROSS_MATS + MIDDLE_MATS
        ]
        results = simple_call(
            finish_kernel, mats + [shape(1, size, F32) for size in vector_sizes]
        )(parts, middle_total, small_all)
        glatent, gq, gkv, gproj, gso, gup, gdn, go = results[:8]
        sums = [row.reshape(-1) for row in results[8:]]
    else:
        cross_grads = jnp.stack([cross_keep, cross_send], 1)
        middle_grads = jnp.stack([middle_keep, middle_send], 1)
        glatent, gq, gkv = scatter_whole(cross_grads, CROSS_MATS)
        gproj, gso, gup, gdn, go = scatter_whole(middle_grads, MIDDLE_MATS)
        total = lax.psum(jnp.concatenate([cross_small, middle_small], 0), axes).reshape(-1)
        sums = [
            total[row * D + start : row * D + start + size]
            for (row, start), size in zip(VECTOR_PLACES, vector_sizes)
        ]

    return (
        latents_out,
        dinput,
        glatent,
        *sums[:4],
        gq,
        sums[4],
        gkv,
        sums[5],
        go,
        *sums[6:9],
        gproj,
        *sums[9:11],
        gso,
        *sums[11:14],
        gup,
        sums[14],
        gdn,
        sums[15],
    )


def solution(mesh):
    rows = P(("wide", "narrow"), None)
    flat = P(("wide", "narrow"))
    block = P("wide", "narrow")
    copied = P()
    return jax.shard_map(
        functools.partial(local, mesh.shape["wide"], mesh.shape["narrow"]),
        mesh=mesh,
        in_specs=(
            rows,
            flat,
            flat,
            rows,
            block,
            copied,
            copied,
            copied,
            copied,
            block,
            copied,
            block,
            copied,
            block,
            copied,
            copied,
            copied,
            block,
            copied,
            copied,
            block,
            copied,
            copied,
            copied,
            block,
            copied,
            block,
            copied,
        ),
        out_specs=(
            rows,
            rows,
            block,
            copied,
            copied,
            copied,
            copied,
            block,
            copied,
            block,
            copied,
            block,
            copied,
            copied,
            copied,
            block,
            copied,
            copied,
            block,
            copied,
            copied,
            copied,
            block,
            copied,
            block,
            copied,
        ),
        check_vma=False,
    )
```
